128 devices in a mesh: grp: 4 (over y), own: 32 (over x, z, core).
Axes of the slice: x: 4, y: 4, z: 4, core: 2. Of those that a mesh axis runs over, the one named last changes fastest.
Arguments:
- user_slot: int32 [4, 128, 128], P(None, ('grp', 'own')), may hold values from 0 to 127, each once within a row
- item_slot: int32 [4, 128, 128], P(None, ('grp', 'own')), may hold values from 0 to 127, each once within a row
- block_counts: int32 [4, 128, 128], P(None, ('grp', 'own')), may hold values from 0 to 1, as said below
- time_gaps: float32 [4, 16384], P(None, ('grp', 'own')), may hold values from -4 to 4
- user_prev: bfloat16 [4, 16384, 512], P(None, ('grp', 'own')), may hold values from -1 to 1
- item_prev: bfloat16 [4, 16384, 512], P(None, ('grp', 'own')), may hold values from -1 to 1
- user_cotangent: float32 [16384, 512], P(('grp', 'own')), may hold values from -6 to 6
- item_cotangent: float32 [16384, 512], P(('grp', 'own')), may hold values from -6 to 6
- user_weight: bfloat16 [1024, 512], replicated, may hold values from -0.1875 to 0.1875
- item_weight: bfloat16 [1024, 512], replicated, may hold values from -0.1875 to 0.1875
- bias_time: float32 [4, 512], replicated, may hold values from -3 to 3
Outputs:
- user_adjoint: float32 [16384, 512], P(('grp', 'own'))
- item_adjoint: float32 [16384, 512], P(('grp', 'own'))
- weight_grads: float32 [2048, 512], P(('grp', 'own'))
- vector_grads: float32 [4, 512], replicated
The draws below stay inside these ranges and needn't reach their ends.
Inputs may be any that keep to these rules, and one draw needn't show every extreme that they name: `user_slot`: each [b, s] row is a permutation, padded rows included. `item_slot`: each [b, p] row is a permutation, padded rows included. block_counts[b, s, p] is the number of live rows from user owner s to item owner p; in every t-batch some item owner receives 1 row from every user owner.
All inputs are finite; a program needn't handle non-finite values.
Results may differ from the reference program's by a relative error of at most 0.0034.
Values sent between devices are 32-bit elements; how exact they have to be, the bound alone decides.
A program may use at most 128 MiB of HBM per device.

```python
import math
import jax
import jax.numpy as jnp
from jax import lax

D = 512
BATCHES = 4
CAP = 1
PEERS = 128
ROWS = 128
N_GRP = 4
N_OWN = 32


def draw_block_counts(key, part):
    key = jax.random.fold_in(key, 11)
    first_key, second_key = jax.random.split(key)
    counts = jax.random.randint(first_key, (BATCHES, PEERS, PEERS), 0, CAP + 1)
    hot_owner = jax.random.randint(second_key, (BATCHES, 1, 1), 0, PEERS)
    columns = jnp.arange(PEERS, dtype=jnp.int32)[None, None, :]
    return jnp.where(columns == hot_owner, CAP, counts).astype(jnp.int32)


def levels(rng, dims, shards, low, largest):
    level = 1.0
    for axis_at, shards_of in shards:
        heights = jax.random.uniform(jax.random.fold_in(jax.random.fold_in(rng, 6), axis_at), (shards_of,), jnp.float32, low / len(shards), largest / len(shards))
        level = level * jnp.repeat(jnp.exp(heights), dims[axis_at] // shards_of).reshape((-1,) + (1,) * (len(dims) - 1 - axis_at))
    return level


def gaussian(key, dims, width, most, pieces=(), kind=jnp.bfloat16):
    entries = jax.random.normal(key, dims, jnp.float32) * width
    if len(pieces) > 0:
        entries = levels(key, dims, pieces, -0.22, 0.18) * entries
    return jnp.clip(entries, min=-most, max=most).astype(kind)


def setup_inputs(seed: int = 0) -> dict:
    seeds = jax.random.split(jax.random.key(seed), 12)
    return {
        "user_slot": jax.vmap(lambda own: jax.random.permutation(own, ROWS))(jax.random.split(seeds[0], BATCHES * PEERS)).reshape((BATCHES, PEERS, ROWS)).astype(jnp.int32),
        "item_slot": jax.vmap(lambda own: jax.random.permutation(own, ROWS))(jax.random.split(seeds[1], BATCHES * PEERS)).reshape((BATCHES, PEERS, ROWS)).astype(jnp.int32),
        "block_counts": draw_block_counts(jax.random.fold_in(seeds[11], 71), 0),
        "time_gaps": gaussian(seeds[3], (BATCHES, PEERS * ROWS), 1.0, 4.0, ((1, 128),), jnp.float32),
        "user_prev": jnp.clip(jax.random.uniform(seeds[4], (BATCHES, PEERS * ROWS, D), jnp.float32, -1.0, 1.0) * levels(seeds[4], (BATCHES, PEERS * ROWS, D), ((1, 128),), -0.4, 0.0), -1.0, 1.0).astype(jnp.bfloat16),
        "item_prev": jnp.clip(jax.random.uniform(seeds[5], (BATCHES, PEERS * ROWS, D), jnp.float32, -1.0, 1.0) * levels(seeds[5], (BATCHES, PEERS * ROWS, D), ((1, 128),), -0.4, 0.0), -1.0, 1.0).astype(jnp.bfloat16),
        "user_cotangent": gaussian(seeds[6], (PEERS * ROWS, D), 1.0, 6.0, ((0, 128),), jnp.float32),
        "item_cotangent": gaussian(seeds[7], (PEERS * ROWS, D), 1.0, 6.0, ((0, 128),), jnp.float32),
        "user_weight": gaussian(seeds[8], (2 * D, D), (2 * D) ** -0.5, 0.1875),
        "item_weight": gaussian(seeds[9], (2 * D, D), (2 * D) ** -0.5, 0.1875),
        "bias_time": gaussian(seeds[10], (4, D), 0.5, 3.0, (), jnp.float32),
    }


def backward_rows(user_rows, item_rows, gap_rows, live_rows, grad_user, grad_item, user_weight, item_weight, bias_time):
    features = user_rows.shape[-1]
    pre_user = jnp.dot(user_rows, user_weight[:features], preferred_element_type=jnp.float32) + jnp.dot(item_rows, user_weight[features:], preferred_element_type=jnp.float32) + gap_rows[:, None] * bias_time[1] + bias_time[0]
    pre_item = jnp.dot(item_rows, item_weight[:features], preferred_element_type=jnp.float32) + jnp.dot(user_rows, item_weight[features:], preferred_element_type=jnp.float32) + gap_rows[:, None] * bias_time[3] + bias_time[2]
    state_user = jnp.tanh(pre_user)
    state_item = jnp.tanh(pre_item)
    live_mask = live_rows.astype(jnp.float32)[:, None]
    delta_user = live_mask * grad_user * (1.0 - state_user * state_user)
    delta_item = live_mask * grad_item * (1.0 - state_item * state_item)
    low_user = delta_user.astype(jnp.bfloat16)
    low_item = delta_item.astype(jnp.bfloat16)
    new_user = jnp.dot(low_user, user_weight[:features].T, preferred_element_type=jnp.float32) + jnp.dot(low_item, item_weight[features:].T, preferred_element_type=jnp.float32)
    new_item = jnp.dot(low_user, user_weight[features:].T, preferred_element_type=jnp.float32) + jnp.dot(low_item, item_weight[:features].T, preferred_element_type=jnp.float32)
    weight_terms = jnp.concatenate([jnp.dot(user_rows.T, low_user, preferred_element_type=jnp.float32), jnp.dot(item_rows.T, low_user, preferred_element_type=jnp.float32), jnp.dot(item_rows.T, low_item, preferred_element_type=jnp.float32), jnp.dot(user_rows.T, low_item, preferred_element_type=jnp.float32)], axis=0)
    vector_terms = jnp.stack([lax.optimization_barrier(jnp.sum(delta_user, axis=0)), lax.optimization_barrier(jnp.sum(gap_rows[:, None] * delta_user, axis=0)), lax.optimization_barrier(jnp.sum(delta_item, axis=0)), lax.optimization_barrier(jnp.sum(gap_rows[:, None] * delta_item, axis=0))], axis=0)
    return (new_user, new_item, weight_terms, vector_terms)

def reference(user_slot, item_slot, block_counts, time_gaps, user_prev, item_prev, user_cotangent, item_cotangent, user_weight, item_weight, bias_time):
    owners = N_GRP * N_OWN
    row_count = CAP * owners
    features = user_prev.shape[-1]
    grad_scale = 1.0 / math.sqrt(BATCHES * owners * row_count)
    adj_users = user_cotangent
    adj_items = item_cotangent
    weight_total = jnp.zeros((4 * features, features), jnp.float32)
    vector_total = jnp.zeros((4, features), jnp.float32)
    offsets = jnp.arange(owners, dtype=jnp.int32) * row_count
    slot_range = jnp.arange(CAP, dtype=jnp.int32)
    for position in range(BATCHES - 1, -1, -1):
        user_index = (user_slot[position] + offsets[:, None]).astype(jnp.int32).reshape(-1)
        item_local = item_slot[position].reshape(owners, owners, CAP)
        item_index = (jnp.transpose(item_local, (1, 0, 2)) + offsets[None, :, None]).astype(jnp.int32).reshape(-1)
        live_rows = (slot_range[None, None, :] < block_counts[position][:, :, None]).reshape(-1)
        grad_user = adj_users[user_index]
        grad_item = adj_items[item_index]
        new_user, new_item, weight_terms, vector_terms = backward_rows(user_prev[position], item_prev[position], time_gaps[position], live_rows, grad_user, grad_item, user_weight, item_weight, bias_time)
        weight_total = weight_total + weight_terms
        vector_total = vector_total + vector_terms
        adj_users = adj_users.at[user_index].set(jnp.where(live_rows[:, None], new_user, grad_user))
        adj_items = adj_items.at[item_index].set(jnp.where(live_rows[:, None], new_item, grad_item))
    return (adj_users, adj_items, weight_total * grad_scale, vector_total * grad_scale)
```

```python
import functools
import math

import jax
import jax.numpy as jnp
from jax import lax
from jax.experimental import pallas as pl
from jax.experimental.pallas import tpu as pltpu
from jax.sharding import PartitionSpec as P

F32 = jnp.float32
BF16 = jnp.bfloat16
MESH = pl.DeviceIdType.MESH

ROWS = 128
D = 512
OWNERS = 128
AUX = 2 * D + 128
WIDE = 384


def device_of(index):
    return (index // 32, index % 32)


def rows_dot(a, b):
    return lax.dot_general(a, b, (((1,), (0,)), ((), ())), preferred_element_type=F32)


def rows_dot_t(a, b):
    return lax.dot_general(a, b, (((1,), (1,)), ((), ())), preferred_element_type=F32)


def permute(onehot, rows):
    high = rows.astype(BF16)
    rest = rows - high.astype(F32)
    middle = rest.astype(BF16)
    low = (rest - middle.astype(F32)).astype(BF16)
    pair = rows_dot(
        jnp.concatenate([onehot, onehot], axis=1), jnp.concatenate([high, middle], axis=0)
    )
    return pair + rows_dot(onehot, low)


def kernel(
    scale,
    user_slot,
    item_slot,
    counts,
    gaps_in,
    user_prev,
    item_prev,
    user_cot,
    item_cot,
    user_weight,
    item_weight,
    bias_time,
    user_out,
    item_out,
    weight_out,
    vector_out,
    v_uslot,
    v_islot,
    v_counts,
    v_gaps,
    v_uprev,
    v_iprev,
    v_ucot,
    v_icot,
    v_uw,
    v_iw,
    v_bias,
    in_sem,
    src,
    dst,
    a2a_send,
    a2a_recv,
    aux_src,
    aux_dst,
    aux_send,
    aux_recv,
    dummy,
    dummy_aux,
    onehots,
    factors,
    prev_t_user,
    prev_t_item,
    low_user_all,
    low_item_all,
    base_user,
    base_item,
    grads_user,
    grads_item,
    live_mine,
    live_here,
    vec,
    vec_core,
    vec_line,
    vec_plane,
    vec_acc,
    weight_acc,
    core_in,
    part_a,
    part_b,
    part_c,
    line_a,
    line_b,
    line_c,
    sum_a,
    sum_b,
    sum_c,
    plane_a,
    plane_b,
    plane_c,
    core_send,
    core_recv,
    line_send,
    line_recv,
    plane_send,
    plane_recv,
):
    grp = lax.axis_index("grp")
    own = lax.axis_index("own")
    me = grp * 32 + own
    my_y = grp
    my_x = own // 8
    my_z = (own // 2) % 4
    my_c = own % 2

    def at(y, x, z, c):
        return (y, x * 8 + z * 2 + c)

    copies = [
        pltpu.make_async_copy(a, b, in_sem.at[i])
        for i, (a, b) in enumerate(
            [
                (item_slot, v_islot),
                (item_cot, v_icot),
                (user_slot, v_uslot),
                (counts, v_counts),
                (gaps_in, v_gaps),
                (user_prev, v_uprev),
                (item_prev, v_iprev),
                (user_weight, v_uw),
                (item_weight, v_iw),
                (bias_time, v_bias),
                (user_cot, v_ucot),
            ]
        )
    ]
    for c in copies:
        c.start()

    barrier = pltpu.get_barrier_semaphore()

    def greet(k, carry):
        pl.semaphore_signal(
            barrier, inc=1, device_id=device_of((me + k) % OWNERS), device_id_type=MESH
        )
        return carry

    lax.fori_loop(1, OWNERS, greet, 0)

    def start_rows(source, target, send_sem, recv_sem):
        def one(k, carry):
            to = (me + k) % OWNERS
            pltpu.make_async_remote_copy(
                src_ref=source.at[pl.ds(to, 1)],
                dst_ref=target.at[pl.ds(me, 1)],
                send_sem=send_sem,
                recv_sem=recv_sem,
                device_id=device_of(to),
                device_id_type=MESH,
            ).start()
            return carry

        lax.fori_loop(1, OWNERS, one, 0)
        target[pl.ds(me, 1)] = source[pl.ds(me, 1)]

    def start_exchange(i):
        start_rows(src.at[i], dst.at[i], a2a_send.at[i], a2a_recv.at[i])

    def wait_bytes(ref, sem):
        pltpu.make_async_copy(ref, ref, sem).wait()

    def arrived(i):
        wait_bytes(dummy.at[pl.ds(0, OWNERS - 1)], a2a_recv.at[i])
        return dst[i]

    def start_aux(i):
        start_rows(aux_src.at[i], aux_dst.at[i], aux_send.at[i], aux_recv.at[i])

    def wait_aux(i):
        wait_bytes(dummy_aux.at[pl.ds(0, OWNERS - 1)], aux_recv.at[i])

    down = lax.broadcasted_iota(jnp.int32, (ROWS, ROWS), 0)
    across = lax.broadcasted_iota(jnp.int32, (ROWS, ROWS), 1)

    def column(row):
        return jnp.sum(jnp.where(down == across, row, 0.0), axis=1, keepdims=True)

    def gather_matrix(slots, b):
        col = column(slots[b].astype(F32))
        return (across.astype(F32) == col).astype(BF16)

    def scatter_matrix(slots, b):
        return (down == slots[b]).astype(BF16)

    def onward_matrix(slots, b):
        return rows_dot(gather_matrix(slots, b), scatter_matrix(slots, b + 1)).astype(BF16)

    copies[0].wait()
    copies[1].wait()
    src[0] = permute(gather_matrix(v_islot, 3), v_icot[...])
    pl.semaphore_wait(barrier, OWNERS - 1)
    start_exchange(0)

    for i in range(3, 7):
        copies[i].wait()

    def fill_aux(i, b):
        aux_src[i, :, 0:D] = v_uprev[b].astype(F32)
        aux_src[i, :, D : 2 * D] = v_iprev[b].astype(F32)
        gap = column(v_gaps[pl.ds(b, 1)])
        live = column((v_counts[b] > 0).astype(F32))
        lane = lax.broadcasted_iota(jnp.int32, (ROWS, 128), 1)
        aux_src[i, :, 2 * D :] = jnp.where(lane == 0, gap, jnp.where(lane == 1, live, 0.0))

    fill_aux(0, 2)
    start_aux(0)

    for i in range(7, 11):
        copies[i].wait()
    copies[2].wait()

    def user_factor(u, i, gap, live):
        pre = (
            rows_dot(u, v_uw[0:D])
            + rows_dot(i, v_uw[D : 2 * D])
            + gap * v_bias[1:2]
            + v_bias[0:1]
        )
        state = jnp.tanh(pre)
        return live * (1.0 - state * state)

    def item_factor(u, i, gap, live):
        pre = (
            rows_dot(i, v_iw[0:D])
            + rows_dot(u, v_iw[D : 2 * D])
            + gap * v_bias[3:4]
            + v_bias[2:3]
        )
        state = jnp.tanh(pre)
        return live * (1.0 - state * state)

    def mine(b):
        gap = column(v_gaps[pl.ds(b, 1)])
        live = column((v_counts[b] > 0).astype(F32))
        return v_uprev[b], v_iprev[b], gap, live

    def here(i):
        u = aux_dst[i, :, 0:D].astype(BF16)
        it = aux_dst[i, :, D : 2 * D].astype(BF16)
        return u, it, aux_dst[i, :, 2 * D : 2 * D + 1], aux_dst[i, :, 2 * D + 1 : 2 * D + 2]

    def keep_transposed(ref, b, u, i, user_first):
        cols = slice(b * ROWS, (b + 1) * ROWS)
        first, second = (u, i) if user_first else (i, u)
        ref[0:D, cols] = first.T
        ref[D : 2 * D, cols] = second.T

    def add_vectors(row, delta, gap):
        vec[row : row + 1] += jnp.sum(delta, axis=0, keepdims=True)
        vec[row + 1 : row + 2] += jnp.sum(gap * delta, axis=0, keepdims=True)

    vec[...] = jnp.zeros_like(vec)

    def keep_low(ref, b, low):
        ref[b * ROWS : (b + 1) * ROWS] = low

    u3, i3, gap3, live3 = mine(3)
    factors[0] = item_factor(u3, i3, gap3, live3)
    grad_user = permute(gather_matrix(v_uslot, 3), v_ucot[...])
    grads_user[...] = grad_user
    delta_user = user_factor(u3, i3, gap3, live3) * grad_user
    low_user = delta_user.astype(BF16)
    keep_low(low_user_all, 3, low_user)
    base_item[...] = rows_dot_t(low_user, v_uw[D : 2 * D])
    base_user[...] = rows_dot_t(low_user, v_uw[0:D])
    add_vectors(0, delta_user, gap3)
    keep_transposed(prev_t_user, 3, u3, i3, True)
    keep_transposed(prev_t_item, 3, u3, i3, False)
    onehots[0] = onward_matrix(v_uslot, 2)
    onehots[1] = onward_matrix(v_islot, 2)
    fill_aux(1, 0)

    grad_item = arrived(0)
    delta_item = factors[0] * grad_item
    low_item = delta_item.astype(BF16)
    new_item = base_item[...] + rows_dot_t(low_item, v_iw[0:D])
    src[1] = jnp.where(live3 > 0.0, new_item, grad_item)
    start_exchange(1)
    new_user = base_user[...] + rows_dot_t(low_item, v_iw[D : 2 * D])
    src[2] = permute(onehots[0], jnp.where(live3 > 0.0, new_user, grads_user[...]))
    start_exchange(2)
    keep_low(low_item_all, 3, low_item)
    add_vectors(2, factors[0] * dst[0], gap3)
    start_aux(1)

    wait_aux(0)
    u2, i2, gap2, live2 = here(0)
    factors[0] = user_factor(u2, i2, gap2, live2)
    factors[1] = item_factor(u2, i2, gap2, live2)
    keep_transposed(prev_t_user, 2, u2, i2, True)
    keep_transposed(prev_t_item, 2, u2, i2, False)
    onehots[2] = onward_matrix(v_uslot, 1)
    onehots[3] = onward_matrix(v_islot, 1)

    grad_item = permute(onehots[1], arrived(1))
    delta_item = factors[1] * grad_item
    low_item = delta_item.astype(BF16)
    grad_user = arrived(2)
    delta_user = factors[0] * grad_user
    low_user = delta_user.astype(BF16)
    new_user = rows_dot_t(low_user, v_uw[0:D]) + rows_dot_t(low_item, v_iw[D : 2 * D])
    src[3] = jnp.where(live2 > 0.0, new_user, grad_user)
    start_exchange(3)
    new_item = rows_dot_t(low_user, v_uw[D : 2 * D]) + rows_dot_t(low_item, v_iw[0:D])
    src[4] = permute(onehots[3], jnp.where(live2 > 0.0, new_item, grad_item))
    start_exchange(4)
    keep_low(low_user_all, 2, low_user)
    keep_low(low_item_all, 2, low_item)
    add_vectors(0, delta_user, gap2)
    add_vectors(2, delta_item, gap2)

    u1, i1, gap1, live1 = mine(1)
    factors[0] = user_factor(u1, i1, gap1, live1)
    factors[1] = item_factor(u1, i1, gap1, live1)
    keep_transposed(prev_t_user, 1, u1, i1, True)
    keep_transposed(prev_t_item, 1, u1, i1, False)
    u0, i0, gap0, live0 = mine(0)
    factors[2] = user_factor(u0, i0, gap0, live0)
    keep_transposed(prev_t_user, 0, u0, i0, True)
    onehots[4] = onward_matrix(v_uslot, 0)
    onehots[5] = onward_matrix(v_islot, 0)

    grad_user = permute(onehots[2], arrived(3))
    delta_user = factors[0] * grad_user
    low_user = delta_user.astype(BF16)
    grad_item = arrived(4)
    delta_item = factors[1] * grad_item
    low_item = delta_item.astype(BF16)
    new_item = rows_dot_t(low_user, v_uw[D : 2 * D]) + rows_dot_t(low_item, v_iw[0:D])
    src[5] = jnp.where(live1 > 0.0, new_item, grad_item)
    start_exchange(5)
    new_user = rows_dot_t(low_user, v_uw[0:D]) + rows_dot_t(low_item, v_iw[D : 2 * D])
    grad_user0 = permute(onehots[4], jnp.where(live1 > 0.0, new_user, grad_user))
    grads_user[...] = grad_user0
    delta_user0 = factors[2] * grad_user0
    low_user0 = delta_user0.astype(BF16)
    src[6] = low_user0.astype(F32)
    start_exchange(6)
    keep_low(low_user_all, 1, low_user)
    keep_low(low_item_all, 1, low_item)
    keep_low(low_user_all, 0, low_user0)
    add_vectors(0, delta_user, gap1)
    add_vectors(2, delta_item, gap1)
    add_vectors(0, delta_user0, gap0)

    sibling = at(my_y, my_x, my_z, 1 - my_c)

    def core_copy(half):
        blocks = pl.ds(half * 32, 32)
        return pltpu.make_async_remote_copy(
            src_ref=weight_acc.at[blocks, 1 - my_c],
            dst_ref=core_in.at[blocks],
            send_sem=core_send.at[half],
            recv_sem=core_recv.at[half],
            device_id=sibling,
            device_id_type=MESH,
        )

    for q in range(4):
        rows = slice(q * 256, (q + 1) * 256)
        weight_acc[q * 8 : (q + 1) * 8] = rows_dot(prev_t_user[rows], low_user_all[...]).reshape(
            8, 2, 16, D
        )
    core_copy(0).start()
    for q in range(4):
        rows = slice(q * 256, (q + 1) * 256)
        weight_acc[32 + q * 8 : 32 + (q + 1) * 8] = rows_dot(
            prev_t_item[rows, ROWS:], low_item_all[ROWS:]
        ).reshape(8, 2, 16, D)

    def add_core(half):
        def one(n, carry):
            y = n // 16
            x = (n // 4) % 4
            z = n % 4
            total = weight_acc[n, my_c] + core_in[n]
            part_a[x, y * 4 + z] = total[0:8, 0:WIDE]
            part_b[y, x * 4 + z] = total[8:16, 0:WIDE]
            part_c[z, y * 4 + x] = total[:, WIDE:]
            return carry

        lax.fori_loop(half * 32, half * 32 + 32, one, 0)

    wait_aux(1)
    u0h, i0h, gap0h, live0h = here(1)
    factors[0] = item_factor(u0h, i0h, gap0h, live0h)
    keep_transposed(prev_t_item, 0, u0h, i0h, False)
    core_copy(0).wait()
    add_core(0)

    grad_item = permute(onehots[5], arrived(5))
    delta_item = factors[0] * grad_item
    low_item0 = delta_item.astype(BF16)
    for q in range(4):
        rows = slice(q * 256, (q + 1) * 256)
        blocks = slice(32 + q * 8, 32 + (q + 1) * 8)
        weight_acc[blocks] += rows_dot(prev_t_item[rows, 0:ROWS], low_item0).reshape(8, 2, 16, D)
    core_copy(1).start()
    add_vectors(2, delta_item, gap0h)
    vec_to_core = pltpu.make_async_remote_copy(
        src_ref=vec,
        dst_ref=vec_core,
        send_sem=core_send.at[2],
        recv_sem=core_recv.at[2],
        device_id=sibling,
        device_id_type=MESH,
    )
    vec_to_core.start()
    src[7] = low_item0.astype(F32)
    start_exchange(7)
    grads_item[...] = grad_item
    core_copy(1).wait()
    add_core(1)
    vec_to_core.wait()
    vec_acc[0] = vec[...] + vec_core[...]

    def line_copies(d):
        x, y, z = (my_x + d) % 4, (my_y + d) % 4, (my_z + d) % 4
        specs = [
            (part_a.at[x], line_a.at[d - 1], at(my_y, x, my_z, my_c)),
            (part_b.at[y], line_b.at[d - 1], at(y, my_x, my_z, my_c)),
            (part_c.at[z], line_c.at[d - 1], at(my_y, my_x, z, my_c)),
            (vec_acc.at[0], vec_line.at[d - 1], at(my_y, x, my_z, my_c)),
        ]
        return [
            pltpu.make_async_remote_copy(
                src_ref=s,
                dst_ref=t,
                send_sem=line_send.at[d - 1, i],
                recv_sem=line_recv.at[d - 1, i],
                device_id=device,
                device_id_type=MESH,
            )
            for i, (s, t, device) in enumerate(specs)
        ]

    lines = [line_copies(d) for d in (2, 1, 3)]
    for group in lines:
        for c in group:
            c.start()

    low_user0h = arrived(6).astype(BF16)
    new_item = rows_dot_t(low_user0h, v_uw[D : 2 * D]) + rows_dot_t(low_item0, v_iw[0:D])
    item_out[...] = permute(
        scatter_matrix(v_islot, 0), jnp.where(live0h > 0.0, new_item, grads_item[...])
    )

    for group in lines:
        for c in group:
            c.wait_recv()
    sum_a[...] = part_a[my_x] + line_a[0] + line_a[1] + line_a[2]
    sum_b[...] = part_b[my_y] + line_b[0] + line_b[1] + line_b[2]
    sum_c[...] = part_c[my_z] + line_c[0] + line_c[1] + line_c[2]
    vec_acc[1] = vec_acc[0] + vec_line[0] + vec_line[1] + vec_line[2]

    def plane_specs(n):
        d, e = n // 4, n % 4
        ay, az = (my_y + d) % 4, (my_z + e) % 4
        bx, bz = (my_x + d) % 4, (my_z + e) % 4
        cy, cx = (my_y + d) % 4, (my_x + e) % 4
        specs = [
            (sum_a.at[ay * 4 + az], plane_a.at[n - 1], at(ay, my_x, az, my_c)),
            (sum_b.at[bx * 4 + bz], plane_b.at[n - 1], at(my_y, bx, bz, my_c)),
            (sum_c.at[cy * 4 + cx], plane_c.at[n - 1], at(cy, cx, my_z, my_c)),
            (vec_acc.at[1], vec_plane.at[n - 1], at(ay, my_x, az, my_c)),
        ]
        return [
            pltpu.make_async_remote_copy(
                src_ref=s,
                dst_ref=t,
                send_sem=plane_send.at[i],
                recv_sem=plane_recv.at[i],
                device_id=device,
                device_id_type=MESH,
            )
            for i, (s, t, device) in enumerate(specs)
        ]

    def start_plane(n, carry):
        for c in plane_specs(n):
            c.start()
        return carry

    lax.fori_loop(1, 16, start_plane, 0)

    low_item0s = arrived(7).astype(BF16)
    low_user0 = low_user_all[0:ROWS]
    new_user = rows_dot_t(low_user0, v_uw[0:D]) + rows_dot_t(low_item0s, v_iw[D : 2 * D])
    live0 = column((v_counts[0] > 0).astype(F32))
    user_out[...] = permute(
        scatter_matrix(v_uslot, 0), jnp.where(live0 > 0.0, new_user, grads_user[...])
    )

    planes = [plane_a, plane_b, plane_c, vec_plane]
    for i, ref in enumerate(planes):
        wait_bytes(ref, plane_recv.at[i])

    def total(own_part, ref):
        result = own_part
        for n in range(15):
            result = result + ref[n]
        return result * scale

    weight_out[0:8, 0:WIDE] = total(sum_a[my_y * 4 + my_z], plane_a)
    weight_out[8:16, 0:WIDE] = total(sum_b[my_x * 4 + my_z], plane_b)
    weight_out[:, WIDE:] = total(sum_c[my_y * 4 + my_x], plane_c)
    vector_out[...] = total(vec_acc[1], vec_plane)[0:4]

    for i in range(8):
        wait_bytes(dummy.at[pl.ds(0, OWNERS - 1)], a2a_send.at[i])
    for i in range(2):
        wait_bytes(dummy_aux.at[pl.ds(0, OWNERS - 1)], aux_send.at[i])
    for group in lines:
        for c in group:
            c.wait_send()
    for i, ref in enumerate(planes):
        wait_bytes(ref, plane_send.at[i])


def per_device(*arrays):
    user_prev = arrays[4]
    batches = user_prev.shape[0]
    scale = 1.0 / math.sqrt(batches * OWNERS * ROWS)
    any_spec = pl.BlockSpec(memory_space=pl.ANY)
    vmem_spec = pl.BlockSpec(memory_space=pltpu.VMEM)
    vmem = pltpu.VMEM
    dma = pltpu.SemaphoreType.DMA
    scratch = [vmem(a.shape, a.dtype) for a in arrays]
    scratch += [
        dma((11,)),
        vmem((8, ROWS, D), F32),
        vmem((8, ROWS, D), F32),
        dma((8,)),
        dma((8,)),
        vmem((2, ROWS, AUX), F32),
        vmem((2, ROWS, AUX), F32),
        dma((2,)),
        dma((2,)),
        vmem((ROWS, 1, D), F32),
        vmem((ROWS, 1, AUX), F32),
        vmem((6, ROWS, ROWS), BF16),
        vmem((3, ROWS, D), F32),
        vmem((2 * D, 4 * ROWS), BF16),
        vmem((2 * D, 4 * ROWS), BF16),
        vmem((4 * ROWS, D), BF16),
        vmem((4 * ROWS, D), BF16),
        vmem((ROWS, D), F32),
        vmem((ROWS, D), F32),
        vmem((ROWS, D), F32),
        vmem((ROWS, D), F32),
        vmem((ROWS, 128), F32),
        vmem((ROWS, 128), F32),
        vmem((8, D), F32),
        vmem((8, D), F32),
        vmem((3, 8, D), F32),
        vmem((15, 8, D), F32),
        vmem((2, 8, D), F32),
        vmem((64, 2, 16, D), F32),
        vmem((64, 16, D), F32),
        vmem((4, 16, 8, WIDE), F32),
        vmem((4, 16, 8, WIDE), F32),
        vmem((4, 16, 16, D - WIDE), F32),
        vmem((3, 16, 8, WIDE), F32),
        vmem((3, 16, 8, WIDE), F32),
        vmem((3, 16, 16, D - WIDE), F32),
        vmem((16, 8, WIDE), F32),
        vmem((16, 8, WIDE), F32),
        vmem((16, 16, D - WIDE), F32),
        vmem((15, 8, WIDE), F32),
        vmem((15, 8, WIDE), F32),
        vmem((15, 16, D - WIDE), F32),
        dma((3,)),
        dma((3,)),
        dma((3, 4)),
        dma((3, 4)),
        dma((4,)),
        dma((4,)),
    ]
    return pl.pallas_call(
        functools.partial(kernel, scale),
        out_shape=(
            jax.ShapeDtypeStruct((ROWS, D), F32),
            jax.ShapeDtypeStruct((ROWS, D), F32),
            jax.ShapeDtypeStruct((16, D), F32),
            jax.ShapeDtypeStruct((4, D), F32),
        ),
        in_specs=[any_spec] * 11,
        out_specs=(vmem_spec,) * 4,
        scratch_shapes=scratch,
        compiler_params=pltpu.CompilerParams(
            collective_id=0, has_side_effects=True, vmem_limit_bytes=56 * 2**20
        ),
        cost_estimate=pl.CostEstimate(
            flops=12_000_000_000, bytes_accessed=5_000_000, transcendentals=600_000
        ),
    )(*arrays)


def solution(mesh):
    both = ("grp", "own")
    in_specs = (
        P(None, both, None),
        P(None, both, None),
        P(None, both, None),
        P(None, both),
        P(None, both, None),
        P(None, both, None),
        P(both, None),
        P(both, None),
        P(),
        P(),
        P(),
    )
    out_specs = (P(both, None), P(both, None), P(both, None), P())
    return jax.shard_map(
        per_device, mesh=mesh, in_specs=in_specs, out_specs=out_specs, check_vma=False
    )
```

```python
import functools
import math

import jax
import jax.numpy as jnp
from jax import lax
from jax.experimental import pallas as pl
from jax.experimental.pallas import tpu as pltpu
from jax.sharding import PartitionSpec as P

F32 = jnp.float32
BF16 = jnp.bfloat16
MESH = pl.DeviceIdType.MESH

ROWS = 128
D = 512
OWNERS = 128
AUX = D + 128
WIDE = 384


def device_of(index):
    return (index // 32, index % 32)


def rows_dot(a, b):
    return lax.dot_general(a, b, (((1,), (0,)), ((), ())), preferred_element_type=F32)


def rows_dot_t(a, b):
    return lax.dot_general(a, b, (((1,), (1,)), ((), ())), preferred_element_type=F32)


def permute(onehot, rows):
    high = rows.astype(BF16)
    rest = rows - high.astype(F32)
    middle = rest.astype(BF16)
    low = (rest - middle.astype(F32)).astype(BF16)
    pair = rows_dot(
        jnp.concatenate([onehot, onehot], axis=1), jnp.concatenate([high, middle], axis=0)
    )
    return pair + rows_dot(onehot, low)


def kernel(
    scale,
    user_slot,
    item_slot,
    counts,
    gaps_in,
    user_prev,
    item_prev,
    user_cot,
    item_cot,
    user_weight,
    item_weight,
    bias_time,
    user_out,
    item_out,
    weight_out,
    vector_out,
    v_uslot,
    v_islot,
    v_counts,
    v_gaps,
    v_uprev,
    v_iprev,
    v_ucot,
    v_icot,
    v_uw,
    v_iw,
    v_bias,
    in_sem,
    src,
    dst,
    a2a_send,
    a2a_recv,
    aux_src,
    aux_dst,
    aux_send,
    aux_recv,
    dummy,
    dummy_aux,
    onehots,
    factors,
    prev_t,
    prev_t_here,
    low_user_all,
    low_item_all,
    base_user,
    base_item,
    grads_user,
    grads_item,
    vec,
    vec_core,
    vec_line,
    vec_plane,
    vec_acc,
    weight_acc,
    core_in,
    part_a,
    part_b,
    part_c,
    line_a,
    line_b,
    line_c,
    sum_a,
    sum_b,
    sum_c,
    plane_a,
    plane_b,
    plane_c,
    core_send,
    core_recv,
    line_send,
    line_recv,
    plane_send,
    plane_recv,
    v_item_out,
    v_user_out,
    out_sem,
):
    grp = lax.axis_index("grp")
    own = lax.axis_index("own")
    me = grp * 32 + own
    my_y = grp
    my_x = own // 8
    my_z = (own // 2) % 4
    my_c = own % 2

    def at(y, x, z, c):
        return (y, x * 8 + z * 2 + c)

    loads = {
        name: pltpu.make_async_copy(a, b, in_sem.at[i])
        for i, (name, a, b) in enumerate(
            [
                ("islot", item_slot, v_islot),
                ("icot", item_cot, v_icot),
                ("counts", counts, v_counts),
                ("gaps", gaps_in, v_gaps),
                ("bias", bias_time, v_bias),
                ("iprev", item_prev, v_iprev),
                ("uprev", user_prev, v_uprev),
                ("iw", item_weight, v_iw),
                ("uw", user_weight, v_uw),
                ("uslot", user_slot, v_uslot),
                ("ucot", user_cot, v_ucot),
            ]
        )
    }
    for load in loads.values():
        load.start()

    barrier = pltpu.get_barrier_semaphore()

    def greet(k, carry):
        pl.semaphore_signal(
            barrier, inc=1, device_id=device_of((me + k) % OWNERS), device_id_type=MESH
        )
        return carry

    lax.fori_loop(1, OWNERS, greet, 0)

    def start_rows(source, target, send_sem, recv_sem):
        def one(k, carry):
            to = (me + k) % OWNERS
            pltpu.make_async_remote_copy(
                src_ref=source.at[pl.ds(to, 1)],
                dst_ref=target.at[pl.ds(me, 1)],
                send_sem=send_sem,
                recv_sem=recv_sem,
                device_id=device_of(to),
                device_id_type=MESH,
            ).start()
            return carry

        lax.fori_loop(1, OWNERS, one, 0)
        target[pl.ds(me, 1)] = source[pl.ds(me, 1)]

    def wait_bytes(ref, sem):
        pltpu.make_async_copy(ref, ref, sem).wait()

    def start_exchange(i):
        start_rows(src.at[i], dst.at[i], a2a_send.at[i], a2a_recv.at[i])

    def arrived(i):
        wait_bytes(dummy.at[pl.ds(0, OWNERS - 1)], a2a_recv.at[i])
        return dst[i]

    def sent(i):
        wait_bytes(dummy.at[pl.ds(0, OWNERS - 1)], a2a_send.at[i])

    def start_aux():
        start_rows(aux_src, aux_dst, aux_send, aux_recv)

    def wait_aux():
        wait_bytes(dummy_aux.at[pl.ds(0, OWNERS - 1)], aux_recv)

    def sent_aux():
        wait_bytes(dummy_aux.at[pl.ds(0, OWNERS - 1)], aux_send)

    down = lax.broadcasted_iota(jnp.int32, (ROWS, ROWS), 0)
    across = lax.broadcasted_iota(jnp.int32, (ROWS, ROWS), 1)

    def column(row):
        return jnp.sum(jnp.where(down == across, row, 0.0), axis=1, keepdims=True)

    def gather_matrix(slots, b):
        col = column(slots[b].astype(F32))
        return (across.astype(F32) == col).astype(BF16)

    def scatter_matrix(slots, b):
        return (down == slots[b]).astype(BF16)

    def onward_matrix(slots, b):
        return rows_dot(gather_matrix(slots, b), scatter_matrix(slots, b + 1)).astype(BF16)

    loads["islot"].wait()
    loads["icot"].wait()
    src[0] = permute(gather_matrix(v_islot, 3), v_icot[...])
    pl.semaphore_wait(barrier, OWNERS - 1)
    start_exchange(0)

    for name in ("counts", "gaps", "bias", "iprev", "uprev", "iw", "uw", "uslot", "ucot"):
        loads[name].wait()

    def user_factor(u, i, gap):
        pre = (
            rows_dot(u, v_uw[0:D])
            + rows_dot(i, v_uw[D : 2 * D])
            + gap * v_bias[1:2]
            + v_bias[0:1]
        )
        state = jnp.tanh(pre)
        return 1.0 - state * state

    def item_factor(u, i, gap):
        pre = (
            rows_dot(i, v_iw[0:D])
            + rows_dot(u, v_iw[D : 2 * D])
            + gap * v_bias[3:4]
            + v_bias[2:3]
        )
        state = jnp.tanh(pre)
        return 1.0 - state * state

    def saved(b):
        gap = column(v_gaps[pl.ds(b, 1)])
        live = column((v_counts[b] > 0).astype(F32))
        return v_uprev[b], v_iprev[b], gap, live

    def keep_transposed(b, u, i):
        prev_t[0:D, b * ROWS : (b + 1) * ROWS] = u.T
        prev_t[D : 2 * D, b * ROWS : (b + 1) * ROWS] = i.T

    def keep_low(ref, b, low):
        ref[b * ROWS : (b + 1) * ROWS] = low

    def add_vectors(row, delta, gap):
        vec[row : row + 1] += jnp.sum(delta, axis=0, keepdims=True)
        vec[row + 1 : row + 2] += jnp.sum(gap * delta, axis=0, keepdims=True)

    vec[...] = jnp.zeros_like(vec)

    u2, i2, gap2, live2 = saved(2)
    src[8] = jnp.where(live2 > 0.0, item_factor(u2, i2, gap2), -1.0)
    start_exchange(8)

    u3, i3, gap3, live3 = saved(3)
    factors[0] = live3 * item_factor(u3, i3, gap3)
    grad_user = permute(gather_matrix(v_uslot, 3), v_ucot[...])
    grads_user[...] = grad_user
    delta_user = live3 * user_factor(u3, i3, gap3) * grad_user
    low_user = delta_user.astype(BF16)
    keep_low(low_user_all, 3, low_user)
    base_item[...] = rows_dot_t(low_user, v_uw[D : 2 * D])
    base_user[...] = rows_dot_t(low_user, v_uw[0:D])
    add_vectors(0, delta_user, gap3)
    factors[1] = live2 * user_factor(u2, i2, gap2)
    onehots[0] = onward_matrix(v_uslot, 2)
    onehots[1] = onward_matrix(v_islot, 2)

    grad_item = arrived(0)
    low_item = (factors[0] * grad_item).astype(BF16)
    new_item = base_item[...] + rows_dot_t(low_item, v_iw[0:D])
    src[1] = jnp.where(live3 > 0.0, new_item, grad_item)
    start_exchange(1)
    new_user = base_user[...] + rows_dot_t(low_item, v_iw[D : 2 * D])
    grad_user = permute(onehots[0], jnp.where(live3 > 0.0, new_user, grads_user[...]))
    delta_user = factors[1] * grad_user
    low_user = delta_user.astype(BF16)
    src[2] = low_user.astype(F32)
    start_exchange(2)
    grads_user[...] = grad_user
    keep_low(low_item_all, 3, low_item)
    keep_low(low_user_all, 2, low_user)
    add_vectors(2, factors[0] * dst[0], gap3)
    add_vectors(0, delta_user, gap2)
    base_user[...] = rows_dot_t(low_user, v_uw[0:D])

    onehots[2] = onward_matrix(v_uslot, 1)
    onehots[3] = onward_matrix(v_islot, 1)
    u1, i1, gap1, live1 = saved(1)
    factors[0] = live1 * user_factor(u1, i1, gap1)
    factors[1] = live1 * item_factor(u1, i1, gap1)
    keep_transposed(3, u3, i3)
    keep_transposed(2, u2, i2)

    src[9] = v_uprev[0].astype(F32)
    start_exchange(9)

    factor = arrived(8)
    grad_item = permute(onehots[1], arrived(1))
    delta_item = jnp.where(factor > -0.5, factor * grad_item, 0.0)
    src[3] = delta_item
    start_exchange(3)
    low_item = delta_item.astype(BF16)
    part = rows_dot_t(low_item, v_iw[0:D])
    low_user = arrived(2).astype(BF16)
    new_item = rows_dot_t(low_user, v_uw[D : 2 * D]) + part
    src[4] = permute(onehots[3], jnp.where(factor > -0.5, new_item, grad_item))
    start_exchange(4)

    u0, i0, gap0, live0 = saved(0)
    lane = lax.broadcasted_iota(jnp.int32, (ROWS, 128), 1)
    aux_src[:, 0:D] = i0.astype(F32)
    aux_src[:, D:] = jnp.where(lane == 0, gap0, jnp.where(lane == 1, live0, 0.0))
    factors[2] = live0 * user_factor(u0, i0, gap0)
    keep_transposed(1, u1, i1)
    keep_transposed(0, u0, i0)
    onehots[4] = onward_matrix(v_uslot, 0)
    onehots[5] = onward_matrix(v_islot, 0)
    start_aux()

    delta_item = arrived(3)
    low_item = delta_item.astype(BF16)
    new_user = base_user[...] + rows_dot_t(low_item, v_iw[D : 2 * D])
    keep_low(low_item_all, 2, low_item)
    grad_user = permute(onehots[2], jnp.where(live2 > 0.0, new_user, grads_user[...]))
    delta_user = factors[0] * grad_user
    low_user = delta_user.astype(BF16)
    keep_low(low_user_all, 1, low_user)
    base_item[...] = rows_dot_t(low_user, v_uw[D : 2 * D])
    base_user[...] = rows_dot_t(low_user, v_uw[0:D])
    grads_user[...] = grad_user
    add_vectors(2, delta_item, gap2)
    add_vectors(0, delta_user, gap1)

    grad_item = arrived(4)
    low_item = (factors[1] * grad_item).astype(BF16)
    new_item = base_item[...] + rows_dot_t(low_item, v_iw[0:D])
    src[5] = jnp.where(live1 > 0.0, new_item, grad_item)
    start_exchange(5)
    new_user = base_user[...] + rows_dot_t(low_item, v_iw[D : 2 * D])
    grad_user = permute(onehots[4], jnp.where(live1 > 0.0, new_user, grads_user[...]))
    delta_user = factors[2] * grad_user
    low_user = delta_user.astype(BF16)
    src[6] = low_user.astype(F32)
    keep_low(low_item_all, 1, low_item)
    keep_low(low_user_all, 0, low_user)
    grads_user[...] = grad_user

    sibling = at(my_y, my_x, my_z, 1 - my_c)

    def core_copy(y):
        blocks = pl.ds(y * 16, 16)
        return pltpu.make_async_remote_copy(
            src_ref=weight_acc.at[blocks, 1 - my_c],
            dst_ref=core_in.at[blocks],
            send_sem=core_send.at[y],
            recv_sem=core_recv.at[y],
            device_id=sibling,
            device_id_type=MESH,
        )

    for q in range(4):
        rows = slice(q * 256, (q + 1) * 256)
        weight_acc[q * 8 : (q + 1) * 8] = rows_dot(prev_t[rows], low_user_all[...]).reshape(
            8, 2, 16, D
        )
    core_copy(0).start()
    core_copy(1).start()
    add_vectors(2, factors[1] * dst[4], gap1)
    add_vectors(0, delta_user, gap0)
    base_user[...] = rows_dot_t(low_user, v_uw[0:D])

    for q in range(4):
        rows = slice(((q + 2) % 4) * 256, ((q + 2) % 4 + 1) * 256)
        weight_acc[32 + q * 8 : 32 + (q + 1) * 8] = rows_dot(
            prev_t[rows, ROWS:], low_item_all[ROWS:]
        ).reshape(8, 2, 16, D)

    start_exchange(6)

    wait_bytes(dummy.at[pl.ds(0, OWNERS - 1)], a2a_recv.at[9])
    wait_aux()
    u0h = dst[9].astype(BF16)
    i0h = aux_dst[:, 0:D].astype(BF16)
    gap0h = aux_dst[:, D : D + 1]
    live0h = aux_dst[:, D + 1 : D + 2]
    factors[0] = live0h * item_factor(u0h, i0h, gap0h)
    prev_t_here[0:D] = i0h.T
    prev_t_here[D : 2 * D] = u0h.T

    def add_core(to_y):
        def one(n, carry):
            x = n // 4
            z = n % 4
            block = to_y * 16 + n
            total = weight_acc[block, my_c] + core_in[block]
            part_a[x, to_y * 4 + z] = total[0:8, 0:WIDE]
            part_b[z, to_y * 4 + x] = total[8:16, 0:WIDE]
            part_c[to_y, x * 4 + z] = total[:, WIDE:]
            return carry

        lax.fori_loop(0, 16, one, 0, unroll=4)

    def line_copy(i, s, t, device):
        return pltpu.make_async_remote_copy(
            src_ref=s,
            dst_ref=t,
            send_sem=line_send.at[i],
            recv_sem=line_recv.at[i],
            device_id=device,
            device_id_type=MESH,
        )

    around = (2, 1, 3)

    def start_lines(to_y):
        rows = pl.ds(to_y * 4, 4)
        for d in around:
            y = (my_y + d) % 4

            @pl.when(y == to_y)
            def _():
                line_copy(
                    2, part_c.at[to_y], line_c.at[d - 1], at(to_y, my_x, my_z, my_c)
                ).start()

        for d in around:
            x, z = (my_x + d) % 4, (my_z + d) % 4
            to_x, to_z = at(my_y, x, my_z, my_c), at(my_y, my_x, z, my_c)
            line_copy(0, part_a.at[x, rows], line_a.at[d - 1, rows], to_x).start()
            line_copy(1, part_b.at[z, rows], line_b.at[d - 1, rows], to_z).start()

    for to_y in (0, 1):
        core_copy(to_y).wait()
        add_core(to_y)
        start_lines(to_y)

    grad_item = permute(onehots[5], arrived(5))
    delta_item = factors[0] * grad_item
    low_item0 = delta_item.astype(BF16)
    for q in range(4):
        rows = slice(q * 256, (q + 1) * 256)
        blocks = slice(32 + q * 8, 32 + (q + 1) * 8)
        weight_acc[blocks] += rows_dot(prev_t_here[rows], low_item0).reshape(8, 2, 16, D)
        if q % 2 == 1:
            core_copy(2 + q // 2).start()
    src[7] = low_item0.astype(F32)
    start_exchange(7)
    add_vectors(2, delta_item, gap0h)
    vec_to_core = pltpu.make_async_remote_copy(
        src_ref=vec,
        dst_ref=vec_core,
        send_sem=core_send.at[4],
        recv_sem=core_recv.at[4],
        device_id=sibling,
        device_id_type=MESH,
    )
    vec_to_core.start()
    grads_item[...] = grad_item
    for to_y in (2, 3):
        core_copy(to_y).wait()
        add_core(to_y)
        start_lines(to_y)
    vec_to_core.wait()
    vec_acc[0] = vec[...] + vec_core[...]
    for d in around:
        to_x = at(my_y, (my_x + d) % 4, my_z, my_c)
        line_copy(3, vec_acc.at[0], vec_line.at[d - 1], to_x).start()

    low_user0h = arrived(6).astype(BF16)
    new_item = rows_dot_t(low_user0h, v_uw[D : 2 * D]) + rows_dot_t(low_item0, v_iw[0:D])
    v_item_out[...] = permute(
        scatter_matrix(v_islot, 0), jnp.where(live0h > 0.0, new_item, grads_item[...])
    )
    item_done = pltpu.make_async_copy(v_item_out, item_out, out_sem.at[0])
    item_done.start()

    line_refs = [line_a, line_b, line_c, vec_line]
    for i, ref in enumerate(line_refs):
        wait_bytes(ref, line_recv.at[i])
    sum_a[...] = part_a[my_x] + line_a[0] + line_a[1] + line_a[2]
    sum_b[...] = part_b[my_z] + line_b[0] + line_b[1] + line_b[2]
    sum_c[...] = part_c[my_y] + line_c[0] + line_c[1] + line_c[2]
    vec_acc[1] = vec_acc[0] + vec_line[0] + vec_line[1] + vec_line[2]

    def start_plane(n, carry):
        d, e = n // 4, n % 4
        ay, az = (my_y + d) % 4, (my_z + e) % 4
        by, bx = (my_y + d) % 4, (my_x + e) % 4
        cx, cz = (my_x + d) % 4, (my_z + e) % 4
        specs = [
            (sum_a.at[ay * 4 + az], plane_a.at[n - 1], at(ay, my_x, az, my_c)),
            (sum_b.at[by * 4 + bx], plane_b.at[n - 1], at(by, bx, my_z, my_c)),
            (sum_c.at[cx * 4 + cz], plane_c.at[n - 1], at(my_y, cx, cz, my_c)),
            (vec_acc.at[1], vec_plane.at[n - 1], at(ay, my_x, az, my_c)),
        ]
        for i, (s, t, device) in enumerate(specs):
            pltpu.make_async_remote_copy(
                src_ref=s,
                dst_ref=t,
                send_sem=plane_send.at[i],
                recv_sem=plane_recv.at[i],
                device_id=device,
                device_id_type=MESH,
            ).start()
        return carry

    lax.fori_loop(1, 16, start_plane, 0)

    low_item0s = arrived(7).astype(BF16)
    new_user = base_user[...] + rows_dot_t(low_item0s, v_iw[D : 2 * D])
    v_user_out[...] = permute(
        scatter_matrix(v_uslot, 0), jnp.where(live0 > 0.0, new_user, grads_user[...])
    )
    user_done = pltpu.make_async_copy(v_user_out, user_out, out_sem.at[1])
    user_done.start()

    planes = [plane_a, plane_b, plane_c, vec_plane]
    for i, ref in enumerate(planes):
        wait_bytes(ref, plane_recv.at[i])

    def total(own_part, ref):
        result = own_part
        for n in range(15):
            result = result + ref[n]
        return result * scale

    weight_out[0:8, 0:WIDE] = total(sum_a[my_y * 4 + my_z], plane_a)
    weight_out[8:16, 0:WIDE] = total(sum_b[my_y * 4 + my_x], plane_b)
    weight_out[:, WIDE:] = total(sum_c[my_x * 4 + my_z], plane_c)
    vector_out[...] = total(vec_acc[1], vec_plane)[0:4]

    item_done.wait()
    user_done.wait()
    for i in range(10):
        sent(i)
    sent_aux()
    for i, ref in enumerate(line_refs):
        wait_bytes(ref, line_send.at[i])
    for i, ref in enumerate(planes):
        wait_bytes(ref, plane_send.at[i])


def hand_over(a, b, c, d, a_out, b_out, c_out, d_out):
    a_out[...] = a[...]
    b_out[...] = b[...]
    c_out[...] = c[...]
    d_out[...] = d[...]


def per_device(*arrays):
    user_prev = arrays[4]
    batches = user_prev.shape[0]
    scale = 1.0 / math.sqrt(batches * OWNERS * ROWS)
    any_spec = pl.BlockSpec(memory_space=pl.ANY)
    vmem_spec = pl.BlockSpec(memory_space=pltpu.VMEM)
    vmem = pltpu.VMEM
    dma = pltpu.SemaphoreType.DMA
    scratch = [vmem(a.shape, a.dtype) for a in arrays]
    scratch += [
        dma((11,)),
        vmem((10, ROWS, D), F32),
        vmem((10, ROWS, D), F32),
        dma((10,)),
        dma((10,)),
        vmem((ROWS, AUX), F32),
        vmem((ROWS, AUX), F32),
        dma,
        dma,
        vmem((ROWS, 1, D), F32),
        vmem((ROWS, 1, AUX), F32),
        vmem((6, ROWS, ROWS), BF16),
        vmem((3, ROWS, D), F32),
        vmem((2 * D, 4 * ROWS), BF16),
        vmem((2 * D, ROWS), BF16),
        vmem((4 * ROWS, D), BF16),
        vmem((4 * ROWS, D), BF16),
        vmem((ROWS, D), F32),
        vmem((ROWS, D), F32),
        vmem((ROWS, D), F32),
        vmem((ROWS, D), F32),
        vmem((8, D), F32),
        vmem((8, D), F32),
        vmem((3, 8, D), F32),
        vmem((15, 8, D), F32),
        vmem((2, 8, D), F32),
        vmem((64, 2, 16, D), F32),
        vmem((64, 16, D), F32),
        vmem((4, 16, 8, WIDE), F32),
        vmem((4, 16, 8, WIDE), F32),
        vmem((4, 16, 16, D - WIDE), F32),
        vmem((3, 16, 8, WIDE), F32),
        vmem((3, 16, 8, WIDE), F32),
        vmem((3, 16, 16, D - WIDE), F32),
        vmem((16, 8, WIDE), F32),
        vmem((16, 8, WIDE), F32),
        vmem((16, 16, D - WIDE), F32),
        vmem((15, 8, WIDE), F32),
        vmem((15, 8, WIDE), F32),
        vmem((15, 16, D - WIDE), F32),
        dma((5,)),
        dma((5,)),
        dma((4,)),
        dma((4,)),
        dma((4,)),
        dma((4,)),
        vmem((ROWS, D), F32),
        vmem((ROWS, D), F32),
        dma((2,)),
    ]
    outputs = pl.pallas_call(
        functools.partial(kernel, scale),
        out_shape=(
            jax.ShapeDtypeStruct((ROWS, D), F32),
            jax.ShapeDtypeStruct((ROWS, D), F32),
            jax.ShapeDtypeStruct((16, D), F32),
            jax.ShapeDtypeStruct((4, D), F32),
        ),
        in_specs=[any_spec] * 11,
        out_specs=(any_spec, any_spec, vmem_spec, vmem_spec),
        scratch_shapes=scratch,
        compiler_params=pltpu.CompilerParams(
            collective_id=0, has_side_effects=True, vmem_limit_bytes=56 * 2**20
        ),
        cost_estimate=pl.CostEstimate(
            flops=12_000_000_000, bytes_accessed=5_000_000, transcendentals=600_000
        ),
    )(*arrays)
    return pl.pallas_call(
        hand_over,
        out_shape=tuple(jax.ShapeDtypeStruct(a.shape, a.dtype) for a in outputs),
        in_specs=[vmem_spec] * 4,
        out_specs=(vmem_spec,) * 4,
    )(*outputs)


def solution(mesh):
    both = ("grp", "own")
    in_specs = (
        P(None, both, None),
        P(None, both, None),
        P(None, both, None),
        P(None, both),
        P(None, both, None),
        P(None, both, None),
        P(both, None),
        P(both, None),
        P(),
        P(),
        P(),
    )
    out_specs = (P(both, None), P(both, None), P(both, None), P())
    return jax.shard_map(
        per_device, mesh=mesh, in_specs=in_specs, out_specs=out_specs, check_vma=False
    )
```

```python
import functools
import math

import jax
import jax.numpy as jnp
from jax import lax
from jax.experimental import pallas as pl
from jax.experimental.pallas import tpu as pltpu
from jax.sharding import PartitionSpec as P

F32 = jnp.float32
BF16 = jnp.bfloat16
MESH = pl.DeviceIdType.MESH

ROWS = 128
D = 512
OWNERS = 128
AUX = D + 128
WIDE = 384


def device_of(index):
    return (index // 32, index % 32)


def rows_dot(a, b):
    return lax.dot_general(a, b, (((1,), (0,)), ((), ())), preferred_element_type=F32)


def rows_dot_t(a, b):
    return lax.dot_general(a, b, (((1,), (1,)), ((), ())), preferred_element_type=F32)


def permute(onehot, rows):
    high = rows.astype(BF16)
    rest = rows - high.astype(F32)
    middle = rest.astype(BF16)
    low = (rest - middle.astype(F32)).astype(BF16)
    pair = rows_dot(
        jnp.concatenate([onehot, onehot], axis=1), jnp.concatenate([high, middle], axis=0)
    )
    return pair + rows_dot(onehot, low)


def kernel(
    scale,
    user_slot,
    item_slot,
    counts,
    gaps_in,
    user_prev,
    item_prev,
    user_cot,
    item_cot,
    user_weight,
    item_weight,
    bias_time,
    user_out,
    item_out,
    weight_out,
    vector_out,
    v_uslot,
    v_islot,
    v_counts,
    v_gaps,
    v_uprev,
    v_iprev,
    v_ucot,
    v_icot,
    v_uw,
    v_iw,
    v_bias,
    in_sem,
    src,
    dst,
    a2a_send,
    a2a_recv,
    aux_src,
    aux_dst,
    aux_send,
    aux_recv,
    dummy,
    dummy_aux,
    onehots,
    factors,
    prev_t,
    prev_t_here,
    low_user_all,
    low_item_all,
    base_user,
    base_item,
    grads_user,
    grads_item,
    vec,
    vec_core,
    vec_line,
    vec_acc,
    vec_send,
    vec_recv,
    weight_acc,
    core_in,
    part_a,
    part_b,
    part_c,
    line_a,
    line_b,
    line_c,
    sum_a,
    sum_b,
    sum_c,
    plane_a,
    plane_b,
    plane_c,
    core_send,
    core_recv,
    line_send,
    line_recv,
    plane_send,
    plane_recv,
    v_item_out,
    v_user_out,
    out_sem,
):
    grp = lax.axis_index("grp")
    own = lax.axis_index("own")
    me = grp * 32 + own
    my_y = grp
    my_x = own // 8
    my_z = (own // 2) % 4
    my_c = own % 2

    def at(y, x, z, c):
        return (y, x * 8 + z * 2 + c)

    loads = {
        name: pltpu.make_async_copy(a, b, in_sem.at[i])
        for i, (name, a, b) in enumerate(
            [
                ("islot", item_slot, v_islot),
                ("icot", item_cot, v_icot),
                ("counts", counts, v_counts),
                ("gaps", gaps_in, v_gaps),
                ("bias", bias_time, v_bias),
                ("iprev", item_prev, v_iprev),
                ("uprev", user_prev, v_uprev),
                ("iw", item_weight, v_iw),
                ("uw", user_weight, v_uw),
                ("uslot", user_slot, v_uslot),
                ("ucot", user_cot, v_ucot),
            ]
        )
    }
    for load in loads.values():
        load.start()

    barrier = pltpu.get_barrier_semaphore()

    def greet(k, carry):
        pl.semaphore_signal(
            barrier, inc=1, device_id=device_of((me + k) % OWNERS), device_id_type=MESH
        )
        return carry

    lax.fori_loop(1, OWNERS, greet, 0)

    def start_rows(source, target, send_sem, recv_sem):
        def one(k, carry):
            to = (me + k) % OWNERS
            pltpu.make_async_remote_copy(
                src_ref=source.at[pl.ds(to, 1)],
                dst_ref=target.at[pl.ds(me, 1)],
                send_sem=send_sem,
                recv_sem=recv_sem,
                device_id=device_of(to),
                device_id_type=MESH,
            ).start()
            return carry

        lax.fori_loop(1, OWNERS, one, 0, unroll=2)
        target[pl.ds(me, 1)] = source[pl.ds(me, 1)]

    def wait_bytes(ref, sem):
        pltpu.make_async_copy(ref, ref, sem).wait()

    def start_exchange(i):
        start_rows(src.at[i], dst.at[i], a2a_send.at[i], a2a_recv.at[i])

    def arrived(i):
        wait_bytes(dummy.at[pl.ds(0, OWNERS - 1)], a2a_recv.at[i])
        return dst[i]

    def sent(i):
        wait_bytes(dummy.at[pl.ds(0, OWNERS - 1)], a2a_send.at[i])

    def start_aux():
        start_rows(aux_src, aux_dst, aux_send, aux_recv)

    def wait_aux():
        wait_bytes(dummy_aux.at[pl.ds(0, OWNERS - 1)], aux_recv)

    def sent_aux():
        wait_bytes(dummy_aux.at[pl.ds(0, OWNERS - 1)], aux_send)

    down = lax.broadcasted_iota(jnp.int32, (ROWS, ROWS), 0)
    across = lax.broadcasted_iota(jnp.int32, (ROWS, ROWS), 1)

    def column(row):
        return jnp.sum(jnp.where(down == across, row, 0.0), axis=1, keepdims=True)

    def gather_matrix(slots, b):
        col = column(slots[b].astype(F32))
        return (across.astype(F32) == col).astype(BF16)

    def scatter_matrix(slots, b):
        return (down == slots[b]).astype(BF16)

    def onward_matrix(slots, b):
        return rows_dot(gather_matrix(slots, b), scatter_matrix(slots, b + 1)).astype(BF16)

    loads["islot"].wait()
    loads["icot"].wait()
    src[0] = permute(gather_matrix(v_islot, 3), v_icot[...])
    pl.semaphore_wait(barrier, OWNERS - 1)
    start_exchange(0)

    for name in ("counts", "gaps", "bias", "iprev", "uprev", "iw", "uw", "uslot", "ucot"):
        loads[name].wait()

    def user_factor(u, i, gap):
        pre = (
            rows_dot(u, v_uw[0:D])
            + rows_dot(i, v_uw[D : 2 * D])
            + gap * v_bias[1:2]
            + v_bias[0:1]
        )
        state = jnp.tanh(pre)
        return 1.0 - state * state

    def item_factor(u, i, gap):
        pre = (
            rows_dot(i, v_iw[0:D])
            + rows_dot(u, v_iw[D : 2 * D])
            + gap * v_bias[3:4]
            + v_bias[2:3]
        )
        state = jnp.tanh(pre)
        return 1.0 - state * state

    def saved(b):
        gap = column(v_gaps[pl.ds(b, 1)])
        live = column((v_counts[b] > 0).astype(F32))
        return v_uprev[b], v_iprev[b], gap, live

    def keep_transposed(b, u, i):
        prev_t[0:D, b * ROWS : (b + 1) * ROWS] = u.T
        prev_t[D : 2 * D, b * ROWS : (b + 1) * ROWS] = i.T

    def keep_low(ref, b, low):
        ref[b * ROWS : (b + 1) * ROWS] = low

    def add_vectors(row, delta, gap):
        vec[row : row + 1] += jnp.sum(delta, axis=0, keepdims=True)
        vec[row + 1 : row + 2] += jnp.sum(gap * delta, axis=0, keepdims=True)

    vec[...] = jnp.zeros_like(vec)

    u2, i2, gap2, live2 = saved(2)
    src[8] = jnp.where(live2 > 0.0, item_factor(u2, i2, gap2), -1.0)
    start_exchange(8)
    src[9] = v_uprev[0].astype(F32)
    start_exchange(9)

    u3, i3, gap3, live3 = saved(3)
    factors[0] = live3 * item_factor(u3, i3, gap3)
    grad_user = permute(gather_matrix(v_uslot, 3), v_ucot[...])
    grads_user[...] = grad_user
    delta_user = live3 * user_factor(u3, i3, gap3) * grad_user
    low_user = delta_user.astype(BF16)
    keep_low(low_user_all, 3, low_user)
    base_item[...] = rows_dot_t(low_user, v_uw[D : 2 * D])
    base_user[...] = rows_dot_t(low_user, v_uw[0:D])
    add_vectors(0, delta_user, gap3)
    factors[1] = live2 * user_factor(u2, i2, gap2)
    onehots[0] = onward_matrix(v_uslot, 2)
    onehots[1] = onward_matrix(v_islot, 2)

    grad_item = arrived(0)
    low_item = (factors[0] * grad_item).astype(BF16)
    new_item = base_item[...] + rows_dot_t(low_item, v_iw[0:D])
    src[1] = jnp.where(live3 > 0.0, new_item, grad_item)
    start_exchange(1)
    new_user = base_user[...] + rows_dot_t(low_item, v_iw[D : 2 * D])
    grad_user = permute(onehots[0], jnp.where(live3 > 0.0, new_user, grads_user[...]))
    delta_user = factors[1] * grad_user
    low_user = delta_user.astype(BF16)
    src[2] = low_user.astype(F32)
    start_exchange(2)
    grads_user[...] = grad_user
    keep_low(low_item_all, 3, low_item)
    keep_low(low_user_all, 2, low_user)
    add_vectors(2, factors[0] * dst[0], gap3)
    add_vectors(0, delta_user, gap2)
    base_user[...] = rows_dot_t(low_user, v_uw[0:D])

    onehots[2] = onward_matrix(v_uslot, 1)
    onehots[3] = onward_matrix(v_islot, 1)
    u1, i1, gap1, live1 = saved(1)
    factors[0] = live1 * user_factor(u1, i1, gap1)
    factors[1] = live1 * item_factor(u1, i1, gap1)
    keep_transposed(3, u3, i3)
    keep_transposed(2, u2, i2)


    factor = arrived(8)
    grad_item = permute(onehots[1], arrived(1))
    delta_item = jnp.where(factor > -0.5, factor * grad_item, 0.0)
    src[3] = delta_item
    start_exchange(3)
    low_item = delta_item.astype(BF16)
    part = rows_dot_t(low_item, v_iw[0:D])
    low_user = arrived(2).astype(BF16)
    new_item = rows_dot_t(low_user, v_uw[D : 2 * D]) + part
    src[4] = permute(onehots[3], jnp.where(factor > -0.5, new_item, grad_item))
    start_exchange(4)

    u0, i0, gap0, live0 = saved(0)
    lane = lax.broadcasted_iota(jnp.int32, (ROWS, 128), 1)
    aux_src[:, 0:D] = i0.astype(F32)
    aux_src[:, D:] = jnp.where(lane == 0, gap0, jnp.where(lane == 1, live0, 0.0))
    factors[2] = live0 * user_factor(u0, i0, gap0)
    keep_transposed(1, u1, i1)
    keep_transposed(0, u0, i0)
    onehots[4] = onward_matrix(v_uslot, 0)
    onehots[5] = onward_matrix(v_islot, 0)
    start_aux()

    delta_item = arrived(3)
    low_item = delta_item.astype(BF16)
    new_user = base_user[...] + rows_dot_t(low_item, v_iw[D : 2 * D])
    keep_low(low_item_all, 2, low_item)
    grad_user = permute(onehots[2], jnp.where(live2 > 0.0, new_user, grads_user[...]))
    delta_user = factors[0] * grad_user
    low_user = delta_user.astype(BF16)
    keep_low(low_user_all, 1, low_user)
    base_item[...] = rows_dot_t(low_user, v_uw[D : 2 * D])
    base_user[...] = rows_dot_t(low_user, v_uw[0:D])
    grads_user[...] = grad_user
    add_vectors(2, delta_item, gap2)
    add_vectors(0, delta_user, gap1)

    grad_item = arrived(4)
    low_item = (factors[1] * grad_item).astype(BF16)
    new_item = base_item[...] + rows_dot_t(low_item, v_iw[0:D])
    src[5] = jnp.where(live1 > 0.0, new_item, grad_item)
    start_exchange(5)
    new_user = base_user[...] + rows_dot_t(low_item, v_iw[D : 2 * D])
    grad_user = permute(onehots[4], jnp.where(live1 > 0.0, new_user, grads_user[...]))
    delta_user = factors[2] * grad_user
    low_user = delta_user.astype(BF16)
    src[6] = low_user.astype(F32)
    keep_low(low_item_all, 1, low_item)
    keep_low(low_user_all, 0, low_user)
    grads_user[...] = grad_user

    sibling = at(my_y, my_x, my_z, 1 - my_c)

    def core_copy(y):
        blocks = pl.ds(y * 16, 16)
        return pltpu.make_async_remote_copy(
            src_ref=weight_acc.at[blocks, 1 - my_c],
            dst_ref=core_in.at[blocks],
            send_sem=core_send.at[y],
            recv_sem=core_recv.at[y],
            device_id=sibling,
            device_id_type=MESH,
        )

    for q in range(4):
        rows = slice(q * 256, (q + 1) * 256)
        weight_acc[q * 8 : (q + 1) * 8] = rows_dot(prev_t[rows], low_user_all[...]).reshape(
            8, 2, 16, D
        )
    core_copy(0).start()
    core_copy(1).start()
    add_vectors(2, factors[1] * dst[4], gap1)
    add_vectors(0, delta_user, gap0)
    base_user[...] = rows_dot_t(low_user, v_uw[0:D])

    for q in range(4):
        rows = slice(((q + 2) % 4) * 256, ((q + 2) % 4 + 1) * 256)
        weight_acc[32 + q * 8 : 32 + (q + 1) * 8] = rows_dot(
            prev_t[rows, ROWS:], low_item_all[ROWS:]
        ).reshape(8, 2, 16, D)


    start_exchange(6)

    wait_bytes(dummy.at[pl.ds(0, OWNERS - 1)], a2a_recv.at[9])
    wait_aux()
    u0h = dst[9].astype(BF16)
    i0h = aux_dst[:, 0:D].astype(BF16)
    gap0h = aux_dst[:, D : D + 1]
    live0h = aux_dst[:, D + 1 : D + 2]
    factors[0] = live0h * item_factor(u0h, i0h, gap0h)
    prev_t_here[0:D] = i0h.T
    prev_t_here[D : 2 * D] = u0h.T

    def add_core(to_y):
        def one(n, carry):
            x = n // 4
            z = n % 4
            block = to_y * 16 + n
            total = weight_acc[block, my_c] + core_in[block]
            part_a[x, to_y * 4 + z] = total[0:8, 0:WIDE]
            part_b[z, to_y * 4 + x] = total[8:16, 0:WIDE]
            part_c[to_y, x * 4 + z] = total[:, WIDE:]
            return carry

        lax.fori_loop(0, 16, one, 0, unroll=4)

    def line_copy(i, s, t, device):
        return pltpu.make_async_remote_copy(
            src_ref=s,
            dst_ref=t,
            send_sem=line_send.at[i],
            recv_sem=line_recv.at[i],
            device_id=device,
            device_id_type=MESH,
        )

    around = (2, 1, 3)

    def start_vec_line(axis):
        for d in around:
            x, y, z = (my_x + d) % 4, (my_y + d) % 4, (my_z + d) % 4
            device = [
                at(my_y, x, my_z, my_c),
                at(y, my_x, my_z, my_c),
                at(my_y, my_x, z, my_c),
            ][axis]
            pltpu.make_async_remote_copy(
                src_ref=vec_acc.at[axis],
                dst_ref=vec_line.at[axis, d - 1],
                send_sem=vec_send.at[axis],
                recv_sem=vec_recv.at[axis],
                device_id=device,
                device_id_type=MESH,
            ).start()

    def add_vec_line(axis):
        wait_bytes(vec_line.at[axis], vec_recv.at[axis])
        vec_acc[axis + 1] = (
            vec_acc[axis] + vec_line[axis, 0] + vec_line[axis, 1] + vec_line[axis, 2]
        )

    def start_lines(to_y):
        rows = pl.ds(to_y * 4, 4)
        for d in around:
            y = (my_y + d) % 4

            @pl.when(y == to_y)
            def _():
                line_copy(
                    2, part_c.at[to_y], line_c.at[d - 1], at(to_y, my_x, my_z, my_c)
                ).start()

        for d in around:
            x, z = (my_x + d) % 4, (my_z + d) % 4
            to_x, to_z = at(my_y, x, my_z, my_c), at(my_y, my_x, z, my_c)
            line_copy(0, part_a.at[x, rows], line_a.at[d - 1, rows], to_x).start()
            line_copy(1, part_b.at[z, rows], line_b.at[d - 1, rows], to_z).start()

    for to_y in (0, 1):
        core_copy(to_y).wait()
        add_core(to_y)
        start_lines(to_y)

    grad_item = permute(onehots[5], arrived(5))
    delta_item = factors[0] * grad_item
    low_item0 = delta_item.astype(BF16)
    for q in range(4):
        rows = slice(q * 256, (q + 1) * 256)
        blocks = slice(32 + q * 8, 32 + (q + 1) * 8)
        weight_acc[blocks] += rows_dot(prev_t_here[rows], low_item0).reshape(8, 2, 16, D)
        if q % 2 == 1:
            core_copy(2 + q // 2).start()
    src[7] = low_item0.astype(F32)
    add_vectors(2, delta_item, gap0h)
    vec_to_core = pltpu.make_async_remote_copy(
        src_ref=vec,
        dst_ref=vec_core,
        send_sem=core_send.at[4],
        recv_sem=core_recv.at[4],
        device_id=sibling,
        device_id_type=MESH,
    )
    vec_to_core.start()
    grads_item[...] = grad_item
    vec_to_core.wait()
    vec_acc[0] = vec[...] + vec_core[...]
    start_vec_line(0)
    for to_y in (2, 3):
        core_copy(to_y).wait()
        add_core(to_y)
        start_lines(to_y)
    start_exchange(7)

    for axis in (1, 2):
        add_vec_line(axis - 1)
        start_vec_line(axis)

    line_refs = [line_a, line_b, line_c]
    for i, ref in enumerate(line_refs):
        wait_bytes(ref, line_recv.at[i])
    sum_a[...] = part_a[my_x] + line_a[0] + line_a[1] + line_a[2]
    sum_b[...] = part_b[my_z] + line_b[0] + line_b[1] + line_b[2]
    sum_c[...] = part_c[my_y] + line_c[0] + line_c[1] + line_c[2]

    def start_plane(n, carry):
        d, e = n // 4, n % 4
        ay, az = (my_y + d) % 4, (my_z + e) % 4
        by, bx = (my_y + d) % 4, (my_x + e) % 4
        cx, cz = (my_x + d) % 4, (my_z + e) % 4
        specs = [
            (sum_a.at[ay * 4 + az], plane_a.at[n - 1], at(ay, my_x, az, my_c)),
            (sum_b.at[by * 4 + bx], plane_b.at[n - 1], at(by, bx, my_z, my_c)),
            (sum_c.at[cx * 4 + cz], plane_c.at[n - 1], at(my_y, cx, cz, my_c)),
        ]
        for i, (s, t, device) in enumerate(specs):
            pltpu.make_async_remote_copy(
                src_ref=s,
                dst_ref=t,
                send_sem=plane_send.at[i],
                recv_sem=plane_recv.at[i],
                device_id=device,
                device_id_type=MESH,
            ).start()
        return carry

    lax.fori_loop(1, 16, start_plane, 0)

    low_item0s = arrived(7).astype(BF16)
    new_user = base_user[...] + rows_dot_t(low_item0s, v_iw[D : 2 * D])
    v_user_out[...] = permute(
        scatter_matrix(v_uslot, 0), jnp.where(live0 > 0.0, new_user, grads_user[...])
    )
    user_done = pltpu.make_async_copy(v_user_out, user_out, out_sem.at[1])
    user_done.start()

    add_vec_line(2)
    vector_out[...] = vec_acc[3, 0:4] * scale

    low_user0h = arrived(6).astype(BF16)
    new_item = rows_dot_t(low_user0h, v_uw[D : 2 * D]) + rows_dot_t(low_item0, v_iw[0:D])
    v_item_out[...] = permute(
        scatter_matrix(v_islot, 0), jnp.where(live0h > 0.0, new_item, grads_item[...])
    )
    item_done = pltpu.make_async_copy(v_item_out, item_out, out_sem.at[0])
    item_done.start()

    planes = [plane_a, plane_b, plane_c]
    for i, ref in enumerate(planes):
        wait_bytes(ref, plane_recv.at[i])

    def total(own_part, ref):
        result = own_part
        for n in range(15):
            result = result + ref[n]
        return result * scale

    weight_out[0:8, 0:WIDE] = total(sum_a[my_y * 4 + my_z], plane_a)
    weight_out[8:16, 0:WIDE] = total(sum_b[my_y * 4 + my_x], plane_b)
    weight_out[:, WIDE:] = total(sum_c[my_x * 4 + my_z], plane_c)

    item_done.wait()
    user_done.wait()
    for i in range(10):
        sent(i)
    sent_aux()
    for i, ref in enumerate(line_refs):
        wait_bytes(ref, line_send.at[i])
    for i in range(3):
        wait_bytes(vec_line.at[i], vec_send.at[i])
    for i, ref in enumerate(planes):
        wait_bytes(ref, plane_send.at[i])


def hand_over(a, b, c, d, a_out, b_out, c_out, d_out):
    a_out[...] = a[...]
    b_out[...] = b[...]
    c_out[...] = c[...]
    d_out[...] = d[...]


def per_device(*arrays):
    user_prev = arrays[4]
    batches = user_prev.shape[0]
    scale = 1.0 / math.sqrt(batches * OWNERS * ROWS)
    any_spec = pl.BlockSpec(memory_space=pl.ANY)
    vmem_spec = pl.BlockSpec(memory_space=pltpu.VMEM)
    vmem = pltpu.VMEM
    dma = pltpu.SemaphoreType.DMA
    scratch = [vmem(a.shape, a.dtype) for a in arrays]
    scratch += [
        dma((11,)),
        vmem((10, ROWS, D), F32),
        vmem((10, ROWS, D), F32),
        dma((10,)),
        dma((10,)),
        vmem((ROWS, AUX), F32),
        vmem((ROWS, AUX), F32),
        dma,
        dma,
        vmem((ROWS, 1, D), F32),
        vmem((ROWS, 1, AUX), F32),
        vmem((6, ROWS, ROWS), BF16),
        vmem((3, ROWS, D), F32),
        vmem((2 * D, 4 * ROWS), BF16),
        vmem((2 * D, ROWS), BF16),
        vmem((4 * ROWS, D), BF16),
        vmem((4 * ROWS, D), BF16),
        vmem((ROWS, D), F32),
        vmem((ROWS, D), F32),
        vmem((ROWS, D), F32),
        vmem((ROWS, D), F32),
        vmem((8, D), F32),
        vmem((8, D), F32),
        vmem((3, 3, 8, D), F32),
        vmem((4, 8, D), F32),
        dma((3,)),
        dma((3,)),
        vmem((64, 2, 16, D), F32),
        vmem((64, 16, D), F32),
        vmem((4, 16, 8, WIDE), F32),
        vmem((4, 16, 8, WIDE), F32),
        vmem((4, 16, 16, D - WIDE), F32),
        vmem((3, 16, 8, WIDE), F32),
        vmem((3, 16, 8, WIDE), F32),
        vmem((3, 16, 16, D - WIDE), F32),
        vmem((16, 8, WIDE), F32),
        vmem((16, 8, WIDE), F32),
        vmem((16, 16, D - WIDE), F32),
        vmem((15, 8, WIDE), F32),
        vmem((15, 8, WIDE), F32),
        vmem((15, 16, D - WIDE), F32),
        dma((5,)),
        dma((5,)),
        dma((3,)),
        dma((3,)),
        dma((3,)),
        dma((3,)),
        vmem((ROWS, D), F32),
        vmem((ROWS, D), F32),
        dma((2,)),
    ]
    outputs = pl.pallas_call(
        functools.partial(kernel, scale),
        out_shape=(
            jax.ShapeDtypeStruct((ROWS, D), F32),
            jax.ShapeDtypeStruct((ROWS, D), F32),
            jax.ShapeDtypeStruct((16, D), F32),
            jax.ShapeDtypeStruct((4, D), F32),
        ),
        in_specs=[any_spec] * 11,
        out_specs=(any_spec, any_spec, vmem_spec, vmem_spec),
        scratch_shapes=scratch,
        compiler_params=pltpu.CompilerParams(
            collective_id=0, has_side_effects=True, vmem_limit_bytes=56 * 2**20
        ),
        cost_estimate=pl.CostEstimate(
            flops=12_000_000_000, bytes_accessed=5_000_000, transcendentals=600_000
        ),
    )(*arrays)
    return pl.pallas_call(
        hand_over,
        out_shape=tuple(jax.ShapeDtypeStruct(a.shape, a.dtype) for a in outputs),
        in_specs=[vmem_spec] * 4,
        out_specs=(vmem_spec,) * 4,
    )(*outputs)


def solution(mesh):
    both = ("grp", "own")
    in_specs = (
        P(None, both, None),
        P(None, both, None),
        P(None, both, None),
        P(None, both),
        P(None, both, None),
        P(None, both, None),
        P(both, None),
        P(both, None),
        P(),
        P(),
        P(),
    )
    out_specs = (P(both, None), P(both, None), P(both, None), P())
    return jax.shard_map(
        per_device, mesh=mesh, in_specs=in_specs, out_specs=out_specs, check_vma=False
    )
```

```python
import functools
import math

import jax
import jax.numpy as jnp
from jax import lax
from jax.experimental import pallas as pl
from jax.experimental.pallas import tpu as pltpu
from jax.sharding import PartitionSpec as P

F32 = jnp.float32
BF16 = jnp.bfloat16
MESH = pl.DeviceIdType.MESH

ROWS = 128
D = 512
OWNERS = 128
AUX = D + 128
WIDE = 384


def device_of(index):
    return (index // 32, index % 32)


def rows_dot(a, b):
    return lax.dot_general(a, b, (((1,), (0,)), ((), ())), preferred_element_type=F32)


def rows_dot_t(a, b):
    return lax.dot_general(a, b, (((1,), (1,)), ((), ())), preferred_element_type=F32)


def permute(onehot, rows):
    high = rows.astype(BF16)
    rest = rows - high.astype(F32)
    middle = rest.astype(BF16)
    low = (rest - middle.astype(F32)).astype(BF16)
    pair = rows_dot(
        jnp.concatenate([onehot, onehot], axis=1), jnp.concatenate([high, middle], axis=0)
    )
    return pair + rows_dot(onehot, low)


def kernel(
    scale,
    user_slot,
    item_slot,
    counts,
    gaps_in,
    user_prev,
    item_prev,
    user_cot,
    item_cot,
    user_weight,
    item_weight,
    bias_time,
    user_out,
    item_out,
    weight_out,
    vector_out,
    v_uslot,
    v_islot,
    v_counts,
    v_gaps,
    v_uprev,
    v_iprev,
    v_ucot,
    v_icot,
    v_uw,
    v_iw,
    v_bias,
    in_sem,
    src,
    dst,
    a2a_send,
    a2a_recv,
    aux_src,
    aux_dst,
    aux_send,
    aux_recv,
    dummy,
    dummy_aux,
    onehots,
    factors,
    prev_t,
    prev_t_here,
    low_user_all,
    low_item_all,
    base_user,
    base_item,
    grads_user,
    grads_item,
    vec,
    vec_core,
    vec_line,
    vec_acc,
    vec_send,
    vec_recv,
    weight_acc,
    core_in,
    part_a,
    part_b,
    part_c,
    line_a,
    line_b,
    line_c,
    sum_a,
    sum_b,
    sum_c,
    plane_a,
    plane_b,
    plane_c,
    core_send,
    core_recv,
    line_send,
    line_recv,
    plane_send,
    plane_recv,
    v_item_out,
    v_user_out,
    out_sem,
):
    grp = lax.axis_index("grp")
    own = lax.axis_index("own")
    me = grp * 32 + own
    my_y = grp
    my_x = own // 8
    my_z = (own // 2) % 4
    my_c = own % 2

    def at(y, x, z, c):
        return (y, x * 8 + z * 2 + c)

    loads = {
        name: pltpu.make_async_copy(a, b, in_sem.at[i])
        for i, (name, a, b) in enumerate(
            [
                ("islot", item_slot, v_islot),
                ("icot", item_cot, v_icot),
                ("counts", counts, v_counts),
                ("gaps", gaps_in, v_gaps),
                ("bias", bias_time, v_bias),
                ("iprev", item_prev, v_iprev),
                ("uprev", user_prev, v_uprev),
                ("iw", item_weight, v_iw),
                ("uw", user_weight, v_uw),
                ("uslot", user_slot, v_uslot),
                ("ucot", user_cot, v_ucot),
            ]
        )
    }
    for load in loads.values():
        load.start()

    barrier = pltpu.get_barrier_semaphore()

    def greet(k, carry):
        pl.semaphore_signal(
            barrier, inc=1, device_id=device_of((me + k) % OWNERS), device_id_type=MESH
        )
        return carry

    lax.fori_loop(1, OWNERS, greet, 0)

    def start_rows(source, target, send_sem, recv_sem):
        def one(k, carry):
            to = (me + k) % OWNERS
            pltpu.make_async_remote_copy(
                src_ref=source.at[pl.ds(to, 1)],
                dst_ref=target.at[pl.ds(me, 1)],
                send_sem=send_sem,
                recv_sem=recv_sem,
                device_id=device_of(to),
                device_id_type=MESH,
            ).start()
            return carry

        lax.fori_loop(1, OWNERS, one, 0, unroll=2)
        target[pl.ds(me, 1)] = source[pl.ds(me, 1)]

    def wait_bytes(ref, sem):
        pltpu.make_async_copy(ref, ref, sem).wait()

    def start_exchange(i):
        start_rows(src.at[i], dst.at[i], a2a_send.at[i], a2a_recv.at[i])

    def arrived(i):
        wait_bytes(dummy.at[pl.ds(0, OWNERS - 1)], a2a_recv.at[i])
        return dst[i]

    def sent(i):
        wait_bytes(dummy.at[pl.ds(0, OWNERS - 1)], a2a_send.at[i])

    def start_aux():
        start_rows(aux_src, aux_dst, aux_send, aux_recv)

    def wait_aux():
        wait_bytes(dummy_aux.at[pl.ds(0, OWNERS - 1)], aux_recv)

    def sent_aux():
        wait_bytes(dummy_aux.at[pl.ds(0, OWNERS - 1)], aux_send)

    down = lax.broadcasted_iota(jnp.int32, (ROWS, ROWS), 0)
    across = lax.broadcasted_iota(jnp.int32, (ROWS, ROWS), 1)

    def column(row):
        return jnp.sum(jnp.where(down == across, row, 0.0), axis=1, keepdims=True)

    def gather_matrix(slots, b):
        col = column(slots[b].astype(F32))
        return (across.astype(F32) == col).astype(BF16)

    def scatter_matrix(slots, b):
        return (down == slots[b]).astype(BF16)

    def onward_matrix(slots, b):
        return rows_dot(gather_matrix(slots, b), scatter_matrix(slots, b + 1)).astype(BF16)

    loads["islot"].wait()
    loads["icot"].wait()
    src[0] = permute(gather_matrix(v_islot, 3), v_icot[...])
    pl.semaphore_wait(barrier, OWNERS - 1)
    start_exchange(0)

    for name in ("counts", "gaps", "bias", "iprev", "uprev", "iw", "uw", "uslot", "ucot"):
        loads[name].wait()

    def user_factor(u, i, gap):
        pre = (
            rows_dot(u, v_uw[0:D])
            + rows_dot(i, v_uw[D : 2 * D])
            + gap * v_bias[1:2]
            + v_bias[0:1]
        )
        state = jnp.tanh(pre)
        return 1.0 - state * state

    def item_factor(u, i, gap):
        pre = (
            rows_dot(i, v_iw[0:D])
            + rows_dot(u, v_iw[D : 2 * D])
            + gap * v_bias[3:4]
            + v_bias[2:3]
        )
        state = jnp.tanh(pre)
        return 1.0 - state * state

    def saved(b):
        gap = column(v_gaps[pl.ds(b, 1)])
        live = column((v_counts[b] > 0).astype(F32))
        return v_uprev[b], v_iprev[b], gap, live

    def keep_transposed(b, u, i):
        prev_t[0:D, b * ROWS : (b + 1) * ROWS] = u.T
        prev_t[D : 2 * D, b * ROWS : (b + 1) * ROWS] = i.T

    def keep_low(ref, b, low):
        ref[b * ROWS : (b + 1) * ROWS] = low

    def add_vectors(row, delta, gap):
        vec[row : row + 1] += jnp.sum(delta, axis=0, keepdims=True)
        vec[row + 1 : row + 2] += jnp.sum(gap * delta, axis=0, keepdims=True)

    vec[...] = jnp.zeros_like(vec)

    u2, i2, gap2, live2 = saved(2)
    src[8] = jnp.where(live2 > 0.0, item_factor(u2, i2, gap2), -1.0)
    start_exchange(8)
    src[9] = v_uprev[0].astype(F32)
    start_exchange(9)

    u3, i3, gap3, live3 = saved(3)
    factors[0] = live3 * item_factor(u3, i3, gap3)
    grad_user = permute(gather_matrix(v_uslot, 3), v_ucot[...])
    grads_user[...] = grad_user
    delta_user = live3 * user_factor(u3, i3, gap3) * grad_user
    low_user = delta_user.astype(BF16)
    keep_low(low_user_all, 3, low_user)
    base_item[...] = rows_dot_t(low_user, v_uw[D : 2 * D])
    base_user[...] = rows_dot_t(low_user, v_uw[0:D])
    add_vectors(0, delta_user, gap3)
    factors[1] = live2 * user_factor(u2, i2, gap2)
    onehots[0] = onward_matrix(v_uslot, 2)
    onehots[1] = onward_matrix(v_islot, 2)

    grad_item = arrived(0)
    low_item = (factors[0] * grad_item).astype(BF16)
    new_item = base_item[...] + rows_dot_t(low_item, v_iw[0:D])
    src[1] = jnp.where(live3 > 0.0, new_item, grad_item)
    start_exchange(1)
    new_user = base_user[...] + rows_dot_t(low_item, v_iw[D : 2 * D])
    grad_user = permute(onehots[0], jnp.where(live3 > 0.0, new_user, grads_user[...]))
    delta_user = factors[1] * grad_user
    low_user = delta_user.astype(BF16)
    src[2] = low_user.astype(F32)
    start_exchange(2)
    grads_user[...] = grad_user
    keep_low(low_item_all, 3, low_item)
    keep_low(low_user_all, 2, low_user)
    add_vectors(2, factors[0] * dst[0], gap3)
    add_vectors(0, delta_user, gap2)
    base_user[...] = rows_dot_t(low_user, v_uw[0:D])

    onehots[2] = onward_matrix(v_uslot, 1)
    onehots[3] = onward_matrix(v_islot, 1)
    u1, i1, gap1, live1 = saved(1)
    factors[0] = live1 * user_factor(u1, i1, gap1)
    factors[1] = live1 * item_factor(u1, i1, gap1)
    keep_transposed(3, u3, i3)
    keep_transposed(2, u2, i2)


    factor = arrived(8)
    grad_item = permute(onehots[1], arrived(1))
    delta_item = jnp.where(factor > -0.5, factor * grad_item, 0.0)
    src[3] = delta_item
    start_exchange(3)
    low_item = delta_item.astype(BF16)
    part = rows_dot_t(low_item, v_iw[0:D])
    low_user = arrived(2).astype(BF16)
    new_item = rows_dot_t(low_user, v_uw[D : 2 * D]) + part
    src[4] = permute(onehots[3], jnp.where(factor > -0.5, new_item, grad_item))
    start_exchange(4)

    u0, i0, gap0, live0 = saved(0)
    lane = lax.broadcasted_iota(jnp.int32, (ROWS, 128), 1)
    aux_src[:, 0:D] = i0.astype(F32)
    aux_src[:, D:] = jnp.where(lane == 0, gap0, jnp.where(lane == 1, live0, 0.0))
    factors[2] = live0 * user_factor(u0, i0, gap0)
    keep_transposed(1, u1, i1)
    keep_transposed(0, u0, i0)
    onehots[4] = onward_matrix(v_uslot, 0)
    onehots[5] = onward_matrix(v_islot, 0)
    start_aux()

    delta_item = arrived(3)
    low_item = delta_item.astype(BF16)
    new_user = base_user[...] + rows_dot_t(low_item, v_iw[D : 2 * D])
    keep_low(low_item_all, 2, low_item)
    grad_user = permute(onehots[2], jnp.where(live2 > 0.0, new_user, grads_user[...]))
    delta_user = factors[0] * grad_user
    low_user = delta_user.astype(BF16)
    keep_low(low_user_all, 1, low_user)
    base_item[...] = rows_dot_t(low_user, v_uw[D : 2 * D])
    base_user[...] = rows_dot_t(low_user, v_uw[0:D])
    grads_user[...] = grad_user
    add_vectors(2, delta_item, gap2)
    add_vectors(0, delta_user, gap1)

    grad_item = arrived(4)
    low_item = (factors[1] * grad_item).astype(BF16)
    new_item = base_item[...] + rows_dot_t(low_item, v_iw[0:D])
    src[5] = jnp.where(live1 > 0.0, new_item, grad_item)
    start_exchange(5)
    new_user = base_user[...] + rows_dot_t(low_item, v_iw[D : 2 * D])
    grad_user = permute(onehots[4], jnp.where(live1 > 0.0, new_user, grads_user[...]))
    delta_user = factors[2] * grad_user
    low_user = delta_user.astype(BF16)
    src[6] = low_user.astype(F32)
    keep_low(low_item_all, 1, low_item)
    keep_low(low_user_all, 0, low_user)
    grads_user[...] = grad_user

    sibling = at(my_y, my_x, my_z, 1 - my_c)

    def core_copy(y):
        blocks = pl.ds(y * 16, 16)
        return pltpu.make_async_remote_copy(
            src_ref=weight_acc.at[blocks, 1 - my_c],
            dst_ref=core_in.at[blocks],
            send_sem=core_send.at[y],
            recv_sem=core_recv.at[y],
            device_id=sibling,
            device_id_type=MESH,
        )

    for q in range(4):
        rows = slice(q * 256, (q + 1) * 256)
        weight_acc[q * 8 : (q + 1) * 8] = rows_dot(prev_t[rows], low_user_all[...]).reshape(
            8, 2, 16, D
        )
    core_copy(0).start()
    core_copy(1).start()
    add_vectors(2, factors[1] * dst[4], gap1)
    add_vectors(0, delta_user, gap0)
    base_user[...] = rows_dot_t(low_user, v_uw[0:D])

    for q in range(4):
        rows = slice(((q + 2) % 4) * 256, ((q + 2) % 4 + 1) * 256)
        weight_acc[32 + q * 8 : 32 + (q + 1) * 8] = rows_dot(
            prev_t[rows, ROWS:], low_item_all[ROWS:]
        ).reshape(8, 2, 16, D)


    start_exchange(6)

    wait_bytes(dummy.at[pl.ds(0, OWNERS - 1)], a2a_recv.at[9])
    wait_aux()
    u0h = dst[9].astype(BF16)
    i0h = aux_dst[:, 0:D].astype(BF16)
    gap0h = aux_dst[:, D : D + 1]
    live0h = aux_dst[:, D + 1 : D + 2]
    factors[0] = live0h * item_factor(u0h, i0h, gap0h)
    prev_t_here[0:D] = i0h.T
    prev_t_here[D : 2 * D] = u0h.T

    def add_core(to_y):
        def one(n, carry):
            x = n // 4
            z = n % 4
            block = to_y * 16 + n
            total = weight_acc[block, my_c] + core_in[block]
            part_a[x, to_y * 4 + z] = total[0:8, 0:WIDE]
            part_b[z, to_y * 4 + x] = total[8:16, 0:WIDE]
            part_c[to_y, x * 4 + z] = total[:, WIDE:]
            return carry

        lax.fori_loop(0, 16, one, 0, unroll=4)

    def line_copy(i, s, t, device):
        return pltpu.make_async_remote_copy(
            src_ref=s,
            dst_ref=t,
            send_sem=line_send.at[i],
            recv_sem=line_recv.at[i],
            device_id=device,
            device_id_type=MESH,
        )

    around = (2, 1, 3)

    def start_vec_line(axis):
        for d in around:
            x, y, z = (my_x + d) % 4, (my_y + d) % 4, (my_z + d) % 4
            device = [
                at(my_y, x, my_z, my_c),
                at(y, my_x, my_z, my_c),
                at(my_y, my_x, z, my_c),
            ][axis]
            pltpu.make_async_remote_copy(
                src_ref=vec_acc.at[axis],
                dst_ref=vec_line.at[axis, d - 1],
                send_sem=vec_send.at[axis],
                recv_sem=vec_recv.at[axis],
                device_id=device,
                device_id_type=MESH,
            ).start()

    def add_vec_line(axis):
        wait_bytes(vec_line.at[axis], vec_recv.at[axis])
        vec_acc[axis + 1] = (
            vec_acc[axis] + vec_line[axis, 0] + vec_line[axis, 1] + vec_line[axis, 2]
        )

    def start_lines(to_y):
        rows = pl.ds(to_y * 4, 4)
        for d in around:
            y = (my_y + d) % 4

            @pl.when(y == to_y)
            def _():
                line_copy(
                    2, part_c.at[to_y], line_c.at[d - 1], at(to_y, my_x, my_z, my_c)
                ).start()

        for d in around:
            x, z = (my_x + d) % 4, (my_z + d) % 4
            to_x, to_z = at(my_y, x, my_z, my_c), at(my_y, my_x, z, my_c)
            line_copy(0, part_a.at[x, rows], line_a.at[d - 1, rows], to_x).start()
            line_copy(1, part_b.at[z, rows], line_b.at[d - 1, rows], to_z).start()

    for to_y in (0, 1):
        core_copy(to_y).wait()
        add_core(to_y)
        start_lines(to_y)

    grad_item = permute(onehots[5], arrived(5))
    delta_item = factors[0] * grad_item
    low_item0 = delta_item.astype(BF16)
    for q in range(4):
        rows = slice(q * 256, (q + 1) * 256)
        blocks = slice(32 + q * 8, 32 + (q + 1) * 8)
        weight_acc[blocks] += rows_dot(prev_t_here[rows], low_item0).reshape(8, 2, 16, D)
        if q % 2 == 1:
            core_copy(2 + q // 2).start()
    src[7] = low_item0.astype(F32)
    add_vectors(2, delta_item, gap0h)
    vec_to_core = pltpu.make_async_remote_copy(
        src_ref=vec,
        dst_ref=vec_core,
        send_sem=core_send.at[4],
        recv_sem=core_recv.at[4],
        device_id=sibling,
        device_id_type=MESH,
    )
    vec_to_core.start()
    grads_item[...] = grad_item
    vec_to_core.wait()
    vec_acc[0] = vec[...] + vec_core[...]
    start_vec_line(0)
    for to_y in (2, 3):
        core_copy(to_y).wait()
        add_core(to_y)
        start_lines(to_y)
    start_exchange(7)

    for axis in (1, 2):
        add_vec_line(axis - 1)
        start_vec_line(axis)

    low_user0h = arrived(6).astype(BF16)
    new_item = rows_dot_t(low_user0h, v_uw[D : 2 * D]) + rows_dot_t(low_item0, v_iw[0:D])
    v_item_out[...] = permute(
        scatter_matrix(v_islot, 0), jnp.where(live0h > 0.0, new_item, grads_item[...])
    )
    item_done = pltpu.make_async_copy(v_item_out, item_out, out_sem.at[0])
    item_done.start()

    line_refs = [line_a, line_b, line_c]
    for i, ref in enumerate(line_refs):
        wait_bytes(ref, line_recv.at[i])
    sum_a[...] = part_a[my_x] + line_a[0] + line_a[1] + line_a[2]
    sum_b[...] = part_b[my_z] + line_b[0] + line_b[1] + line_b[2]
    sum_c[...] = part_c[my_y] + line_c[0] + line_c[1] + line_c[2]

    def start_plane(n, carry):
        d, e = n // 4, n % 4
        ay, az = (my_y + d) % 4, (my_z + e) % 4
        by, bx = (my_y + d) % 4, (my_x + e) % 4
        cx, cz = (my_x + d) % 4, (my_z + e) % 4
        specs = [
            (sum_a.at[ay * 4 + az], plane_a.at[n - 1], at(ay, my_x, az, my_c)),
            (sum_b.at[by * 4 + bx], plane_b.at[n - 1], at(by, bx, my_z, my_c)),
            (sum_c.at[cx * 4 + cz], plane_c.at[n - 1], at(my_y, cx, cz, my_c)),
        ]
        for i, (s, t, device) in enumerate(specs):
            pltpu.make_async_remote_copy(
                src_ref=s,
                dst_ref=t,
                send_sem=plane_send.at[i],
                recv_sem=plane_recv.at[i],
                device_id=device,
                device_id_type=MESH,
            ).start()
        return carry

    lax.fori_loop(1, 16, start_plane, 0)

    low_item0s = arrived(7).astype(BF16)
    new_user = base_user[...] + rows_dot_t(low_item0s, v_iw[D : 2 * D])
    v_user_out[...] = permute(
        scatter_matrix(v_uslot, 0), jnp.where(live0 > 0.0, new_user, grads_user[...])
    )
    user_done = pltpu.make_async_copy(v_user_out, user_out, out_sem.at[1])
    user_done.start()

    add_vec_line(2)
    vector_out[...] = vec_acc[3, 0:4] * scale

    planes = [plane_a, plane_b, plane_c]
    for i, ref in enumerate(planes):
        wait_bytes(ref, plane_recv.at[i])

    def total(own_part, ref):
        result = own_part
        for n in range(15):
            result = result + ref[n]
        return result * scale

    weight_out[0:8, 0:WIDE] = total(sum_a[my_y * 4 + my_z], plane_a)
    weight_out[8:16, 0:WIDE] = total(sum_b[my_y * 4 + my_x], plane_b)
    weight_out[:, WIDE:] = total(sum_c[my_x * 4 + my_z], plane_c)

    item_done.wait()
    user_done.wait()
    for i in range(10):
        sent(i)
    sent_aux()
    for i, ref in enumerate(line_refs):
        wait_bytes(ref, line_send.at[i])
    for i in range(3):
        wait_bytes(vec_line.at[i], vec_send.at[i])
    for i, ref in enumerate(planes):
        wait_bytes(ref, plane_send.at[i])


def hand_over(a, b, c, d, a_out, b_out, c_out, d_out):
    a_out[...] = a[...]
    b_out[...] = b[...]
    c_out[...] = c[...]
    d_out[...] = d[...]


def per_device(*arrays):
    user_prev = arrays[4]
    batches = user_prev.shape[0]
    scale = 1.0 / math.sqrt(batches * OWNERS * ROWS)
    any_spec = pl.BlockSpec(memory_space=pl.ANY)
    vmem_spec = pl.BlockSpec(memory_space=pltpu.VMEM)
    vmem = pltpu.VMEM
    dma = pltpu.SemaphoreType.DMA
    scratch = [vmem(a.shape, a.dtype) for a in arrays]
    scratch += [
        dma((11,)),
        vmem((10, ROWS, D), F32),
        vmem((10, ROWS, D), F32),
        dma((10,)),
        dma((10,)),
        vmem((ROWS, AUX), F32),
        vmem((ROWS, AUX), F32),
        dma,
        dma,
        vmem((ROWS, 1, D), F32),
        vmem((ROWS, 1, AUX), F32),
        vmem((6, ROWS, ROWS), BF16),
        vmem((3, ROWS, D), F32),
        vmem((2 * D, 4 * ROWS), BF16),
        vmem((2 * D, ROWS), BF16),
        vmem((4 * ROWS, D), BF16),
        vmem((4 * ROWS, D), BF16),
        vmem((ROWS, D), F32),
        vmem((ROWS, D), F32),
        vmem((ROWS, D), F32),
        vmem((ROWS, D), F32),
        vmem((8, D), F32),
        vmem((8, D), F32),
        vmem((3, 3, 8, D), F32),
        vmem((4, 8, D), F32),
        dma((3,)),
        dma((3,)),
        vmem((64, 2, 16, D), F32),
        vmem((64, 16, D), F32),
        vmem((4, 16, 8, WIDE), F32),
        vmem((4, 16, 8, WIDE), F32),
        vmem((4, 16, 16, D - WIDE), F32),
        vmem((3, 16, 8, WIDE), F32),
        vmem((3, 16, 8, WIDE), F32),
        vmem((3, 16, 16, D - WIDE), F32),
        vmem((16, 8, WIDE), F32),
        vmem((16, 8, WIDE), F32),
        vmem((16, 16, D - WIDE), F32),
        vmem((15, 8, WIDE), F32),
        vmem((15, 8, WIDE), F32),
        vmem((15, 16, D - WIDE), F32),
        dma((5,)),
        dma((5,)),
        dma((3,)),
        dma((3,)),
        dma((3,)),
        dma((3,)),
        vmem((ROWS, D), F32),
        vmem((ROWS, D), F32),
        dma((2,)),
    ]
    outputs = pl.pallas_call(
        functools.partial(kernel, scale),
        out_shape=(
            jax.ShapeDtypeStruct((ROWS, D), F32),
            jax.ShapeDtypeStruct((ROWS, D), F32),
            jax.ShapeDtypeStruct((16, D), F32),
            jax.ShapeDtypeStruct((4, D), F32),
        ),
        in_specs=[any_spec] * 11,
        out_specs=(any_spec, any_spec, vmem_spec, vmem_spec),
        scratch_shapes=scratch,
        compiler_params=pltpu.CompilerParams(
            collective_id=0, has_side_effects=True, vmem_limit_bytes=56 * 2**20
        ),
        cost_estimate=pl.CostEstimate(
            flops=12_000_000_000, bytes_accessed=5_000_000, transcendentals=600_000
        ),
    )(*arrays)
    return pl.pallas_call(
        hand_over,
        out_shape=tuple(jax.ShapeDtypeStruct(a.shape, a.dtype) for a in outputs),
        in_specs=[vmem_spec] * 4,
        out_specs=(vmem_spec,) * 4,
    )(*outputs)


def solution(mesh):
    both = ("grp", "own")
    in_specs = (
        P(None, both, None),
        P(None, both, None),
        P(None, both, None),
        P(None, both),
        P(None, both, None),
        P(None, both, None),
        P(both, None),
        P(both, None),
        P(),
        P(),
        P(),
    )
    out_specs = (P(both, None), P(both, None), P(both, None), P())
    return jax.shard_map(
        per_device, mesh=mesh, in_specs=in_specs, out_specs=out_specs, check_vma=False
    )
```
